32 devices in a mesh: dp: 8 (over z, x), row: 2 (over y), col: 2 (over core).
Axes of the slice: x: 2, y: 2, z: 4, core: 2. Of those that a mesh axis runs over, the one named last changes fastest.
Arguments:
- latents: bfloat16 [16384, 1152], P(('dp', 'row'), 'col'), may hold values from -6 to 6
- skip_input: bfloat16 [16384, 1152], P(('dp', 'row'), 'col'), may hold values from -6 to 6
- condition: bfloat16 [16, 1152], P('dp', 'col'), may hold values from -6 to 6
- text_states: bfloat16 [5328, 1024], P(('dp', 'col'), 'row'), may hold values from -6 to 6
- positions: int32 [16384, 2], P(('dp', 'row')), may hold values from 0 to 63, as said below
- cotangent: bfloat16 [16384, 1152], P(('dp', 'col'), 'row'), may hold values from -6 to 6
- skip_gain: float32 [2, 1152], P(None, 'col'), may hold values from 0.1 to 1.9
- skip_weight: bfloat16 [2, 1152, 1152], P(None, 'col', 'row'), may hold values from -0.125 to 0.125
- shift_weight: bfloat16 [1152, 1152], P('col', 'row'), may hold values from -0.1875 to 0.1875
- self_gain: float32 [1152], P('row'), may hold values from 0.1 to 1.9
- self_weight: bfloat16 [1152, 3, 1152], P('row', None, 'col'), may hold values from -0.1875 to 0.1875
- query_gain: float32 [72], replicated, may hold values from 0.1 to 1.9
- key_gain: float32 [72], replicated, may hold values from 0.1 to 1.9
- self_out: bfloat16 [1152, 1152], P('col', 'row'), may hold values from -0.3125 to 0.3125
- cross_gain: float32 [1152], P('row'), may hold values from 0.1 to 1.9
- cross_query: bfloat16 [1152, 1152], P('row', 'col'), may hold values from -1 to 1
- cross_context: bfloat16 [1024, 2, 1152], P('row', None, 'col'), may hold values from -0.1875 to 0.1875
- cross_query_gain: float32 [72], replicated, may hold values from 0.1 to 1.9
- cross_key_gain: float32 [72], replicated, may hold values from 0.1 to 1.9
- cross_out: bfloat16 [1152, 1152], P('col', 'row'), may hold values from -0.625 to 0.625
- feed_gain: float32 [1152], P('row'), may hold values from 0.1 to 1.9
- up_weight: bfloat16 [1152, 4608], P('row', 'col'), may hold values from -1 to 1
- down_weight: bfloat16 [4608, 1152], P('col', 'row'), may hold values from -0.09375 to 0.09375
Outputs:
- block_out: bfloat16 [16384, 1152], P(('dp', 'col'), 'row')
- grad_latents: bfloat16 [16384, 1152], P(('dp', 'row'), 'col')
- grad_skip_input: bfloat16 [16384, 1152], P(('dp', 'row'), 'col')
- grad_text_states: bfloat16 [5328, 1024], P(('dp', 'col'), 'row')
- grad_skip_gain: float32 [2, 1152], P(None, 'col')
- grad_skip_weight: float32 [2, 1152, 1152], P(None, 'col', 'row')
- grad_shift_weight: float32 [1152, 1152], P('col', 'row')
- grad_self_gain: float32 [1152], P('row')
- grad_self_weight: float32 [1152, 3, 1152], P('row', None, 'col')
- grad_query_gain: float32 [72], replicated
- grad_key_gain: float32 [72], replicated
- grad_self_out: float32 [1152, 1152], P('col', 'row')
- grad_cross_gain: float32 [1152], P('row')
- grad_cross_query: float32 [1152, 1152], P('row', 'col')
- grad_cross_context: float32 [1024, 2, 1152], P('row', None, 'col')
- grad_cross_query_gain: float32 [72], replicated
- grad_cross_key_gain: float32 [72], replicated
- grad_cross_out: float32 [1152, 1152], P('col', 'row')
- grad_feed_gain: float32 [1152], P('row')
- grad_up_weight: float32 [1152, 4608], P('row', 'col')
- grad_down_weight: float32 [4608, 1152], P('col', 'row')
The draws below stay inside these ranges and needn't reach their ends.
Inputs may be any that keep to these rules, and one draw needn't show every extreme that they name: `positions`: within each image of 1024 latent tokens, token i stands at (i // w, i % w) for a width w drawn per image from 16, 32 and 64.
All inputs are finite; a program needn't handle non-finite values.
Results may differ from the reference program's by a relative error of at most 0.02.
Values may be sent and summed in bfloat16 or wider, within the bound.
A program may use at most 256 MiB of HBM per device.

```python
import jax
import jax.numpy as jnp
from jax import lax

D = 1152
HEADS = 16
HD = 72
FF = 4608
CTX = 1024
TXT = 333
SIDE = 32
LAT = 1024
SEQ_ALL = 16
TOKENS = 16384
TEXT_ROWS = 5328


def draw_positions(key, part):
    key = jax.random.fold_in(key, 11)
    sequence_count = TOKENS // LAT
    shapes_drawn = jax.random.randint(key, (sequence_count,), 0, 3).astype(jnp.int32)
    shapes_drawn = shapes_drawn.at[0].set(0)
    heights = SIDE // 2 * jnp.left_shift(jnp.int32(1), shapes_drawn)
    widths = LAT // heights
    places = jnp.arange(LAT, dtype=jnp.int32)
    grid_rows = places[None, :] // widths[:, None]
    grid_cols = places[None, :] % widths[:, None]
    return jnp.stack([grid_rows, grid_cols], axis=-1).reshape(TOKENS, 2).astype(jnp.int32)


def draw_up_weight(key, part):
    key = jax.random.fold_in(key, 23)
    base_key = jax.random.fold_in(key, 1)
    offset_key = jax.random.fold_in(key, 2)
    base = jnp.clip(jax.random.normal(base_key, (D, FF), jnp.float32), -4.0, 4.0)
    offset = 1.5 * jnp.clip(jax.random.normal(offset_key, (FF,), jnp.float32), -2.0, 2.0)
    return ((base + offset[None, :]) * D ** (-0.5)).astype(jnp.bfloat16)


def draw_cross_query(key, part):
    key = jax.random.fold_in(key, 29)
    base_key = jax.random.fold_in(key, 1)
    offset_key = jax.random.fold_in(key, 2)
    base = jnp.clip(jax.random.normal(base_key, (D, D), jnp.float32), -4.0, 4.0)
    offset = 1.5 * jnp.clip(jax.random.normal(offset_key, (D,), jnp.float32), -2.0, 2.0)
    return ((base + offset[None, :]) * D ** (-0.5)).astype(jnp.bfloat16)


def block_scale(stream_key, shape, shards, least, high):
    def one(dim, parts):
        draws = jax.random.uniform(jax.random.fold_in(jax.random.fold_in(stream_key, 6), dim), (parts,), jnp.float32, least / len(shards), high / len(shards))
        return jnp.repeat(jnp.exp(draws), shape[dim] // parts).reshape((-1,) + (1,) * (len(shape) - dim - 1))

    factor_of = one(*shards[0])
    for cut in shards[1:]:
        factor_of = factor_of * one(*cut)
    return factor_of


def scatter_about(key, extent, spread, reach, pieces=(), held_as=jnp.bfloat16):
    drawn = jax.random.normal(key, extent, jnp.float32) * spread
    if len(pieces) > 0:
        drawn = block_scale(key, extent, pieces, -0.22, 0.18) * drawn
    return jnp.clip(drawn, min=-reach, max=reach).astype(held_as)


def setup_inputs(seed: int = 0) -> dict:
    key_of = jax.random.split(jax.random.key(seed), 24)
    return {
        "latents": scatter_about(key_of[0], (TOKENS, D), 1.0, 6.0, ((0, 16), (1, 2))),
        "skip_input": scatter_about(key_of[1], (TOKENS, D), 1.0, 6.0, ((0, 16), (1, 2))),
        "condition": scatter_about(key_of[2], (SEQ_ALL, D), 1.0, 6.0, ((0, 8), (1, 2))),
        "text_states": scatter_about(key_of[3], (TEXT_ROWS, CTX), 1.0, 6.0, ((0, 16), (1, 2))),
        "positions": draw_positions(jax.random.fold_in(key_of[23], 71), 0),
        "cotangent": scatter_about(key_of[5], (TOKENS, D), 1.0, 6.0, ((0, 16), (1, 2))),
        "skip_gain": jnp.clip(1.0 + 0.18 * jax.random.normal(key_of[6], (2, D), jnp.float32), 0.1, 1.9),
        "skip_weight": scatter_about(key_of[7], (2, D, D), (2 * D) ** -0.5, 0.125, ((1, 2), (2, 2))),
        "shift_weight": scatter_about(key_of[8], (D, D), D ** -0.5, 0.1875, ((0, 2), (1, 2))),
        "self_gain": jnp.clip(1.0 + 0.18 * jax.random.normal(key_of[9], (D,), jnp.float32), 0.1, 1.9),
        "self_weight": scatter_about(key_of[10], (D, 3, D), D ** -0.5, 0.1875, ((0, 2), (2, 2))),
        "query_gain": jnp.clip(1.0 + 0.18 * jax.random.normal(key_of[11], (HD,), jnp.float32), 0.1, 1.9),
        "key_gain": jnp.clip(1.0 + 0.18 * jax.random.normal(key_of[12], (HD,), jnp.float32), 0.1, 1.9),
        "self_out": scatter_about(key_of[13], (D, D), (D // 3) ** -0.5, 0.3125, ((0, 2), (1, 2))),
        "cross_gain": jnp.clip(1.0 + 0.18 * jax.random.normal(key_of[14], (D,), jnp.float32), 0.1, 1.9),
        "cross_query": draw_cross_query(jax.random.fold_in(key_of[23], 71), 0),
        "cross_context": scatter_about(key_of[16], (CTX, 2, D), CTX ** -0.5, 0.1875, ((0, 2), (2, 2))),
        "cross_query_gain": jnp.clip(1.0 + 0.18 * jax.random.normal(key_of[17], (HD,), jnp.float32), 0.1, 1.9),
        "cross_key_gain": jnp.clip(1.0 + 0.18 * jax.random.normal(key_of[18], (HD,), jnp.float32), 0.1, 1.9),
        "cross_out": scatter_about(key_of[19], (D, D), (max(D // 12, 1)) ** -0.5, 0.625, ((0, 2), (1, 2))),
        "feed_gain": jnp.clip(1.0 + 0.18 * jax.random.normal(key_of[20], (D,), jnp.float32), 0.1, 1.9),
        "up_weight": draw_up_weight(jax.random.fold_in(key_of[23], 71), 0),
        "down_weight": scatter_about(key_of[22], (FF, D), FF ** -0.5, 0.09375, ((0, 2), (1, 2))),
    }


EPSILON = 1e-06
PRECISE = lax.Precision.HIGHEST

@jax.custom_vjp
def low(v):
    return lax.optimization_barrier(v.astype(jnp.bfloat16)).astype(jnp.float32)

@jax.custom_vjp
def low_back(v):
    return v

def low_keep(v):
    return (low(v), None)

def low_pass(kept, grad):
    return (grad,)

def back_keep(v):
    return (v, None)

def back_low(kept, grad):
    return (low(grad),)
low.defvjp(low_keep, low_pass)
low_back.defvjp(back_keep, back_low)

def matmul(left_side, right_side):
    return jnp.dot(left_side, right_side, precision=PRECISE)

def layer_norm(values, norm_gain):
    average = lax.optimization_barrier(jnp.mean(values, axis=-1, keepdims=True))
    variance = lax.optimization_barrier(jnp.mean(values * values, axis=-1, keepdims=True)) - average * average
    return (values - average) * lax.rsqrt(variance + EPSILON) * norm_gain

def rotate(values, row_place, col_place):
    half_width = values.shape[-1] // 2
    quarter = half_width // 2
    frequency = 10000.0 ** (-jnp.arange(quarter, dtype=jnp.float32) / quarter)

    def turn_half(portion, place):
        angles = place[:, None] * frequency[None, :]
        cosine = jnp.cos(angles)[:, None, :]
        sine_value = jnp.sin(angles)[:, None, :]
        leading = portion[..., :quarter]
        trailing = portion[..., quarter:]
        return jnp.concatenate([leading * cosine - trailing * sine_value, trailing * cosine + leading * sine_value], axis=-1)
    return jnp.concatenate([turn_half(values[..., :half_width], row_place), turn_half(values[..., half_width:], col_place)], axis=-1)

def attend(queries, key_rows, value_rows):
    query_len = queries.shape[0]
    block_len = min(512, query_len)
    blocks = queries.reshape(query_len // block_len, block_len, queries.shape[1], queries.shape[2])
    score_scale = queries.shape[2] ** (-0.5)

    def one_block(query_block):
        scores = jnp.einsum('qhe,khe->hqk', query_block, key_rows, precision=PRECISE) * score_scale
        weights_full = jax.nn.softmax(low_back(scores), axis=-1)
        return jnp.einsum('hqk,khe->qhe', low(weights_full), value_rows, precision=PRECISE)
    return lax.map(jax.checkpoint(one_block), blocks).reshape(queries.shape)

def forward_one(latent_rows, skip_rows, cond_row, text_rows, row_place, col_place, params):
    skip_gain, skip_weight, shift_weight, self_gain, self_weight, query_gain, key_gain, self_out, cross_gain, cross_query, cross_context, cross_query_gain, cross_key_gain, cross_out, feed_gain, up_weight, down_weight = params
    joined = jnp.concatenate([latent_rows, skip_rows], axis=-1)
    skip_low = low(layer_norm(joined, skip_gain.reshape(2 * D)))
    first_state = low_back(matmul(skip_low, skip_weight.reshape(2 * D, D)))
    shift_row = matmul(low(jax.nn.silu(cond_row))[None, :], shift_weight)
    first_input = low(layer_norm(first_state, self_gain) + shift_row)
    mixed_raw = low_back(matmul(first_input, self_weight.reshape(D, 3 * D))).reshape(LAT, 3, HEADS, HD)
    queries = low(rotate(layer_norm(mixed_raw[:, 0], query_gain), row_place, col_place))
    key_rows = low(rotate(layer_norm(mixed_raw[:, 1], key_gain), row_place, col_place))
    value_rows = low(mixed_raw[:, 2])
    heads_low = low(low_back(attend(queries, key_rows, value_rows))).reshape(LAT, D)
    second_state = first_state + low_back(matmul(heads_low, self_out))
    cross_input = low(layer_norm(second_state, cross_gain))
    probe_raw = low_back(matmul(cross_input, cross_query)).reshape(LAT, HEADS, HD)
    probes = low(layer_norm(probe_raw, cross_query_gain))
    memory = low_back(matmul(text_rows, cross_context.reshape(CTX, 2 * D))).reshape(TXT, 2, HEADS, HD)
    memory_keys = low(layer_norm(memory[:, 0], cross_key_gain))
    memory_values = low(memory[:, 1])
    cross_low = low(low_back(attend(probes, memory_keys, memory_values))).reshape(LAT, D)
    third_state = second_state + low_back(matmul(cross_low, cross_out))
    feed_input = low(layer_norm(third_state, feed_gain))
    hidden_raw = low_back(matmul(feed_input, up_weight))
    hidden_low = low(jax.nn.gelu(hidden_raw, approximate=True))
    return third_state + low_back(matmul(hidden_low, down_weight))

def reference(latents, skip_input, condition, text_states, positions, cotangent, skip_gain, skip_weight, shift_weight, self_gain, self_weight, query_gain, key_gain, self_out, cross_gain, cross_query, cross_context, cross_query_gain, cross_key_gain, cross_out, feed_gain, up_weight, down_weight):
    params = tuple((weight.astype(jnp.float32) for weight in (skip_gain, skip_weight, shift_weight, self_gain, self_weight, query_gain, key_gain, self_out, cross_gain, cross_query, cross_context, cross_query_gain, cross_key_gain, cross_out, feed_gain, up_weight, down_weight)))
    seq_total = condition.shape[0]
    sequences = (latents.astype(jnp.float32).reshape(seq_total, LAT, D), skip_input.astype(jnp.float32).reshape(seq_total, LAT, D), condition.astype(jnp.float32), text_states.astype(jnp.float32).reshape(seq_total, TXT, CTX), positions.astype(jnp.float32).reshape(seq_total, LAT, 2), cotangent.astype(jnp.float32).reshape(seq_total, LAT, D))

    def one_sequence(running, sequence):
        latent_rows, skip_rows, cond_row, text_rows, places, cot_rows = sequence

        def forward_here(latent_part, skip_part, text_part, *weights):
            return forward_one(latent_part, skip_part, cond_row, text_part, places[:, 0], places[:, 1], weights)
        result, pullback = jax.vjp(forward_here, latent_rows, skip_rows, text_rows, *params)
        gradients = pullback(cot_rows)
        updated = tuple((summed + gradient for summed, gradient in zip(running, gradients[3:])))
        return (updated, (result, gradients[0], gradients[1], gradients[2]))
    zero_grads = tuple((jnp.zeros_like(weight) for weight in params))
    grad_sums, outputs = lax.scan(one_sequence, zero_grads, sequences)
    block_out = outputs[0].reshape(TOKENS, D).astype(jnp.bfloat16)
    grad_latents = outputs[1].reshape(TOKENS, D).astype(jnp.bfloat16)
    grad_skip_input = outputs[2].reshape(TOKENS, D).astype(jnp.bfloat16)
    grad_text_states = outputs[3].reshape(TEXT_ROWS, CTX).astype(jnp.bfloat16)
    return (block_out, grad_latents, grad_skip_input, grad_text_states, grad_sums[0], grad_sums[1], grad_sums[2], grad_sums[3], grad_sums[4], grad_sums[5], grad_sums[6], grad_sums[7], grad_sums[8], grad_sums[9], grad_sums[10], grad_sums[11], grad_sums[12], grad_sums[13], grad_sums[14], grad_sums[15], grad_sums[16])
```

```python
import jax
import jax.numpy as jnp
from jax import lax
from jax.sharding import PartitionSpec as P

D = 1152
HD = 72
TXT = 333
LAT = 1024


EPSILON = 1e-06
PRECISE = lax.Precision.HIGHEST
SWAP = [(0, 1), (1, 0)]
BF16 = jnp.bfloat16
F32 = jnp.float32


def other_core(values):
    return lax.ppermute(values, "col", SWAP)


def other_chip(values):
    return lax.ppermute(values, "row", SWAP)


def contract(left_side, right_side, transposed=False):
    numbers = (((1,), (1 if transposed else 0,)), ((), ()))
    return lax.dot_general(left_side, right_side, numbers, preferred_element_type=F32)


def token_sum(left_side, right_side):
    return lax.dot_general(
        left_side, right_side, (((0,), (0,)), ((), ())), preferred_element_type=F32
    )


def both_halves(own, weight, transposed=False):
    other = other_core(own)
    product = jnp.concatenate(
        [contract(own, weight, transposed), contract(other, weight, transposed)]
    )
    return product, jnp.concatenate([own, other])


def own_half(values, weight, transposed=False):
    half = values.shape[0] // 2
    sent = contract(values[half:], weight, transposed)
    return contract(values[:half], weight, transposed) + other_core(sent)


def after(values, earlier):
    return lax.optimization_barrier((values, earlier))[0]


def head_norm(values, norm_gain):
    average = jnp.mean(values, axis=-1, keepdims=True)
    variance = jnp.mean(values * values, axis=-1, keepdims=True) - average * average
    return (values - average) * lax.rsqrt(variance + EPSILON) * norm_gain


def gelu_tanh(values):
    return jax.nn.gelu(values, approximate=True)


def rotate(values, row_place, col_place):
    half_width = values.shape[-1] // 2
    quarter = half_width // 2
    frequency = 10000.0 ** (-jnp.arange(quarter, dtype=jnp.float32) / quarter)

    def turn_half(portion, place):
        angles = place[:, None] * frequency[None, :]
        cosine = jnp.cos(angles)[:, None, :]
        sine_value = jnp.sin(angles)[:, None, :]
        leading = portion[..., :quarter]
        trailing = portion[..., quarter:]
        return jnp.concatenate(
            [leading * cosine - trailing * sine_value, trailing * cosine + leading * sine_value],
            axis=-1,
        )

    return jnp.concatenate(
        [
            turn_half(values[..., :half_width], row_place),
            turn_half(values[..., half_width:], col_place),
        ],
        axis=-1,
    )


def norm_rows(values):
    average = jnp.mean(values, axis=1, keepdims=True)
    variance = jnp.mean(values * values, axis=1, keepdims=True) - average * average
    inverse = lax.rsqrt(variance + EPSILON)
    return ((values - average) * inverse, inverse)


def norm_rows_back(grad_normed, normed, inverse, norm_gain):
    scaled = grad_normed * norm_gain
    first_mean = jnp.mean(scaled, axis=1, keepdims=True)
    second_mean = jnp.mean(scaled * normed, axis=1, keepdims=True)
    grad_input = inverse * (scaled - first_mean - normed * second_mean)
    return (grad_input, jnp.sum(grad_normed * normed, axis=0))


def attend_forward(queries, key_rows, value_rows, key_len, first_row, block_len):
    heads_here = queries.shape[1]
    head_width = queries.shape[2]
    score_scale = head_width ** (-0.5)
    groups = key_rows.shape[0] // key_len
    key_groups = key_rows.reshape(groups, key_len, heads_here, head_width)
    value_groups = value_rows.reshape(groups, key_len, heads_here, head_width)
    block_count = queries.shape[0] // block_len
    query_blocks = queries.reshape(block_count, block_len, heads_here, head_width)
    block_ids = jnp.arange(block_count, dtype=jnp.int32)

    def one_block(packed):
        block_id, query_block = packed
        group_index = (first_row + block_id * block_len) // LAT
        key_block = lax.dynamic_index_in_dim(key_groups, group_index, 0, keepdims=False)
        value_block = lax.dynamic_index_in_dim(value_groups, group_index, 0, keepdims=False)
        scores = (
            jnp.einsum("qhe,khe->hqk", query_block, key_block, preferred_element_type=jnp.float32)
            * score_scale
        )
        row_top = jnp.max(scores, axis=-1, keepdims=True)
        row_total = jnp.sum(jnp.exp(scores - row_top), axis=-1, keepdims=True)
        log_total = row_top + jnp.log(row_total)
        weights_low = jnp.exp(scores - log_total).astype(jnp.bfloat16)
        output = jnp.einsum(
            "hqk,khe->qhe", weights_low, value_block, preferred_element_type=jnp.float32
        )
        return (output, log_total[..., 0])

    outputs, log_totals = lax.map(one_block, (block_ids, query_blocks))
    return (outputs.reshape(queries.shape), log_totals)


def attend_backward(
    queries, key_rows, value_rows, grad_heads, log_totals, key_len, first_row, block_len
):
    heads_here = queries.shape[1]
    head_width = queries.shape[2]
    score_scale = head_width ** (-0.5)
    groups = key_rows.shape[0] // key_len
    key_groups = key_rows.reshape(groups, key_len, heads_here, head_width)
    value_groups = value_rows.reshape(groups, key_len, heads_here, head_width)
    block_count = queries.shape[0] // block_len
    query_blocks = queries.reshape(block_count, block_len, heads_here, head_width)
    grad_blocks = grad_heads.reshape(block_count, block_len, heads_here, head_width)
    block_ids = jnp.arange(block_count, dtype=jnp.int32)

    def one_block(carry, packed):
        key_store, value_store = carry
        block_id, query_block, grad_block, log_block = packed
        group_index = (first_row + block_id * block_len) // LAT
        key_block = lax.dynamic_index_in_dim(key_groups, group_index, 0, keepdims=False)
        value_block = lax.dynamic_index_in_dim(value_groups, group_index, 0, keepdims=False)
        scores = (
            jnp.einsum("qhe,khe->hqk", query_block, key_block, preferred_element_type=jnp.float32)
            * score_scale
        )
        weights_full = jnp.exp(scores - log_block[..., None])
        grad_weights = jnp.einsum(
            "qhe,khe->hqk", grad_block, value_block, preferred_element_type=jnp.float32
        )
        inner_sum = jnp.sum(weights_full * grad_weights, axis=-1, keepdims=True)
        grad_scores = (weights_full * (grad_weights - inner_sum)).astype(jnp.bfloat16)
        grad_query = (
            jnp.einsum("hqk,khe->qhe", grad_scores, key_block, preferred_element_type=jnp.float32)
            * score_scale
        )
        grad_key = (
            jnp.einsum("hqk,qhe->khe", grad_scores, query_block, preferred_element_type=jnp.float32)
            * score_scale
        )
        grad_value = jnp.einsum(
            "hqk,qhe->khe",
            weights_full.astype(jnp.bfloat16),
            grad_block,
            preferred_element_type=jnp.float32,
        )
        key_now = lax.dynamic_index_in_dim(key_store, group_index, 0, keepdims=False) + grad_key
        value_now = (
            lax.dynamic_index_in_dim(value_store, group_index, 0, keepdims=False) + grad_value
        )
        key_store = lax.dynamic_update_index_in_dim(key_store, key_now, group_index, 0)
        value_store = lax.dynamic_update_index_in_dim(value_store, value_now, group_index, 0)
        return ((key_store, value_store), grad_query)

    empty = jnp.zeros((groups, key_len, heads_here, head_width), jnp.float32)
    (key_store, value_store), grad_query = lax.scan(
        one_block, (empty, empty), (block_ids, query_blocks, grad_blocks, log_totals)
    )
    return (
        grad_query.reshape(queries.shape),
        key_store.reshape(key_rows.shape),
        value_store.reshape(value_rows.shape),
    )


def shards(
    latents,
    skip_input,
    condition,
    text_states,
    positions,
    cotangent,
    skip_gain,
    skip_weight,
    shift_weight,
    self_gain,
    self_weight,
    query_gain,
    key_gain,
    self_out,
    cross_gain,
    cross_query,
    cross_context,
    cross_query_gain,
    cross_key_gain,
    cross_out,
    feed_gain,
    up_weight,
    down_weight,
):
    tokens, width = latents.shape
    half = tokens // 2
    heads_here = width // HD
    core = lax.axis_index("col")
    chip = lax.axis_index("row")
    straight = core == chip

    def own_first(values):
        return (
            lax.dynamic_slice_in_dim(values, core * half, half, 0),
            lax.dynamic_slice_in_dim(values, (1 - core) * half, half, 0),
        )

    def in_order(own, other):
        return jnp.where(
            core == 0, jnp.concatenate([own, other]), jnp.concatenate([other, own])
        )

    skip_flat = skip_weight.reshape(2 * width, -1)
    self_flat = self_weight.reshape(-1, 3 * width)
    context_flat = cross_context.reshape(-1, 2 * width)

    def whole(weight, axis):
        return jnp.concatenate([weight, other_chip(weight)], axis=axis)

    skip_all = whole(skip_flat, 1)
    self_all = whole(self_flat, 0)
    self_out_all = whole(self_out, 1)
    context_all = whole(context_flat, 0)
    query_all = whole(cross_query, 0)
    cross_out_all = whole(cross_out, 1)
    up_all = whole(up_weight, 0)
    down_all = whole(down_weight, 1)
    norm_gains = jnp.stack([self_gain, cross_gain, feed_gain])
    norm_gains = jnp.concatenate([norm_gains, other_chip(norm_gains)], axis=1)
    self_gain_all, cross_gain_all, feed_gain_all = norm_gains[0], norm_gains[1], norm_gains[2]

    text_near = other_core(text_states)
    text_mine = jnp.where(straight, text_states, text_near)
    text_far = other_chip(jnp.where(straight, text_near, text_states))
    text_all = jnp.concatenate([text_mine, text_far], axis=1)
    kept, handed = own_first(cotangent)
    handed = other_core(handed)
    cot_mine = jnp.where(straight, kept, handed)
    cot_far = other_chip(jnp.where(straight, handed, kept))
    cot_own = jnp.concatenate([cot_mine, cot_far], axis=1)

    place_own, place_other = own_first(positions)
    places = jnp.concatenate([place_own, place_other]).astype(F32)
    row_place = places[:, 0]
    col_place = places[:, 1]
    block_len = min(512, LAT)

    lat_own, lat_other = own_first(latents)
    skip_own, skip_other = own_first(skip_input)
    joined = jnp.stack(
        [jnp.concatenate([lat_own, lat_other]), jnp.concatenate([skip_own, skip_other])], axis=1
    ).astype(F32)
    sums = jnp.stack([jnp.sum(joined, axis=(1, 2)), jnp.sum(joined * joined, axis=(1, 2))])

    def swap_halves(values):
        return jnp.concatenate([values[:, half:], values[:, :half]], axis=1)

    sums = sums + swap_halves(other_core(sums))
    average = sums[0] / (2 * D)
    variance = sums[1] / (2 * D) - average * average
    skip_inverse = lax.rsqrt(variance + EPSILON)
    skip_normed = (joined - average[:, None, None]) * skip_inverse[:, None, None]
    skip_low = (skip_normed * skip_gain).astype(BF16).reshape(tokens, 2 * width)
    first_state = own_half(skip_low, skip_all)

    cond_low = jax.nn.silu(condition.astype(F32)).astype(BF16)
    shift_part = contract(cond_low, shift_weight)
    shift_part = shift_part + other_core(shift_part)
    shift_mine = lax.dynamic_slice_in_dim(shift_part, chip, 1, 0)
    shift_far = other_chip(lax.dynamic_slice_in_dim(shift_part, 1 - chip, 1, 0))
    shift_row = jnp.concatenate([shift_mine, shift_far], axis=1)

    normed_one, inverse_one = norm_rows(first_state)
    first_input = (normed_one * self_gain_all + shift_row).astype(BF16)
    mixed_raw, first_all = both_halves(first_input, self_all)
    mixed_raw = mixed_raw.reshape(tokens, 3, heads_here, HD)

    def shape_query(raw_part, norm_gain):
        return rotate(head_norm(raw_part, norm_gain), row_place, col_place)

    query_float, query_pull = jax.vjp(shape_query, mixed_raw[:, 0], query_gain)
    key_float, key_pull = jax.vjp(shape_query, mixed_raw[:, 1], key_gain)
    queries = query_float.astype(BF16)
    key_rows = key_float.astype(BF16)
    value_rows = mixed_raw[:, 2].astype(BF16)
    heads_float, log_first = attend_forward(queries, key_rows, value_rows, LAT, 0, block_len)
    heads_low = heads_float.astype(BF16).reshape(tokens, width)
    second_state = first_state + own_half(heads_low, self_out_all)

    normed_two, inverse_two = norm_rows(second_state)
    cross_input = (normed_two * cross_gain_all).astype(BF16)
    probe_raw, cross_all = both_halves(cross_input, query_all)
    probe_raw = probe_raw.reshape(tokens, heads_here, HD)
    memory_raw = contract(text_all, context_all)
    text_here = memory_raw.shape[0]
    memory_raw = memory_raw.reshape(text_here, 2, heads_here, HD)
    probe_float, probe_pull = jax.vjp(head_norm, probe_raw, cross_query_gain)
    memory_float, memory_pull = jax.vjp(head_norm, memory_raw[:, 0], cross_key_gain)
    probes = probe_float.astype(BF16)
    memory_keys = memory_float.astype(BF16)
    memory_values = memory_raw[:, 1].astype(BF16)
    cross_float, log_second = attend_forward(probes, memory_keys, memory_values, TXT, 0, block_len)
    cross_low = cross_float.astype(BF16).reshape(tokens, width)
    third_state = second_state + own_half(cross_low, cross_out_all)

    normed_three, inverse_three = norm_rows(third_state)
    feed_input = (normed_three * feed_gain_all).astype(BF16)
    hidden_raw, feed_all = both_halves(feed_input, up_all)
    hidden_float, gelu_pull = jax.vjp(gelu_tanh, hidden_raw)
    hidden_low = hidden_float.astype(BF16)
    out_own = (third_state + own_half(hidden_low, down_all)).astype(BF16)
    row_width = up_weight.shape[0]
    out_mine = out_own[:, :row_width]
    out_far = other_chip(out_own[:, row_width:])
    out_kept = jnp.where(straight, out_mine, out_far)
    out_got = other_core(jnp.where(straight, out_far, out_mine))
    block_out = in_order(out_kept, out_got)

    grad_hidden, cot_all = both_halves(cot_own, down_all, True)
    grad_down = token_sum(hidden_low, cot_all)
    grad_pre = gelu_pull(grad_hidden)[0].astype(BF16)
    grad_up = token_sum(feed_all, grad_pre)
    grad_feed_in = own_half(grad_pre, up_all, True)
    back_three, feed_gain_part = norm_rows_back(
        grad_feed_in, normed_three, inverse_three, feed_gain_all
    )
    grad_third = cot_own.astype(F32) + back_three

    branch_two = grad_third.astype(BF16)
    grad_cross_heads, branch_two_all = both_halves(branch_two, cross_out_all, True)
    grad_cross_out = token_sum(cross_low, branch_two_all)
    grad_cross_low = grad_cross_heads.astype(BF16).reshape(tokens, heads_here, HD)
    grad_probe, grad_memory_key, grad_memory_value = attend_backward(
        probes, memory_keys, memory_values, grad_cross_low, log_second, TXT, 0, block_len
    )
    grad_probe_raw, grad_probe_gain = probe_pull(grad_probe)
    probe_low = grad_probe_raw.astype(BF16).reshape(tokens, width)
    grad_cross_query = token_sum(cross_all, probe_low)
    grad_cross_in = own_half(probe_low, query_all, True)
    grad_memory_raw, grad_memory_gain = memory_pull(grad_memory_key)
    memory_low = jnp.stack([grad_memory_raw, grad_memory_value], axis=1).astype(BF16)
    memory_low = memory_low.reshape(text_here, 2 * width)
    grad_context = token_sum(text_all, memory_low)
    text_part = contract(memory_low, context_all, True)
    text_width = text_states.shape[1]
    text_one, text_two = text_part[:, :text_width], text_part[:, text_width:]
    text_sum = jnp.where(straight, text_one, text_two) + other_core(
        jnp.where(straight, text_two, text_one)
    )
    text_sum = text_sum.astype(BF16)
    text_back = lax.ppermute(text_sum, ("row", "col"), [(1, 2), (2, 1)])
    grad_text_states = jnp.where(straight, text_sum, text_back)

    back_two, cross_gain_part = norm_rows_back(
        grad_cross_in, normed_two, inverse_two, cross_gain_all
    )
    grad_second = grad_third + back_two
    branch_one = grad_second.astype(BF16)
    grad_heads, branch_one_all = both_halves(branch_one, self_out_all, True)
    grad_self_out = token_sum(heads_low, branch_one_all)
    grad_heads_low = grad_heads.astype(BF16).reshape(tokens, heads_here, HD)
    grad_query, grad_key, grad_value = attend_backward(
        queries, key_rows, value_rows, grad_heads_low, log_first, LAT, 0, block_len
    )
    grad_query_raw, grad_query_gain = query_pull(grad_query)
    grad_key_raw, grad_key_gain = key_pull(grad_key)
    mixed_low = jnp.stack([grad_query_raw, grad_key_raw, grad_value], axis=1).astype(BF16)
    mixed_low = mixed_low.reshape(tokens, 3 * width)
    grad_self_weight = token_sum(first_all, mixed_low)
    grad_first_in = own_half(mixed_low, self_all, True)

    shift_grad = jnp.sum(grad_first_in, axis=0, keepdims=True)
    shift_grad = shift_grad + other_core(shift_grad)
    shift_here = shift_grad[:, :row_width]
    shift_there = other_chip(shift_grad[:, row_width:])
    shift_pair = jnp.where(
        chip == 0,
        jnp.concatenate([shift_here, shift_there]),
        jnp.concatenate([shift_there, shift_here]),
    )
    cond_every = lax.all_gather(cond_low, "dp", axis=0, tiled=True)
    shift_every = lax.all_gather(shift_pair, "dp", axis=0, tiled=True)
    grad_shift_weight = lax.dot_general(
        cond_every.astype(F32),
        shift_every,
        (((0,), (0,)), ((), ())),
        precision=PRECISE,
        preferred_element_type=F32,
    )

    back_one, self_gain_part = norm_rows_back(grad_first_in, normed_one, inverse_one, self_gain_all)
    grad_first = grad_second + back_one
    grad_skip_out, grad_first_all = both_halves(grad_first.astype(BF16), skip_all, True)
    grad_skip_weight = token_sum(skip_low, grad_first_all)
    grad_joined_out = grad_skip_out.reshape(tokens, 2, width)
    scaled = grad_joined_out * skip_gain
    sums_back = jnp.stack(
        [jnp.sum(scaled, axis=(1, 2)), jnp.sum(scaled * skip_normed, axis=(1, 2))]
    )
    sums_back = sums_back + swap_halves(other_core(sums_back))
    first_mean = (sums_back[0] / (2 * D))[:, None, None]
    second_mean = (sums_back[1] / (2 * D))[:, None, None]
    grad_joined = skip_inverse[:, None, None] * (scaled - first_mean - skip_normed * second_mean)
    skip_gain_part = jnp.sum(grad_joined_out * skip_normed, axis=0)
    grad_joined = grad_joined.astype(BF16)
    grad_latents = in_order(grad_joined[:half, 0], grad_joined[half:, 0])
    grad_skip_input = in_order(grad_joined[:half, 1], grad_joined[half:, 1])

    wide = jnp.stack([self_gain_part, cross_gain_part, feed_gain_part])
    wide = wide + other_core(wide)
    narrow = jnp.stack([grad_query_gain, grad_key_gain, grad_probe_gain, grad_memory_gain])
    narrow = narrow + other_core(narrow)

    def flat(*pieces):
        return jnp.concatenate([piece.reshape(-1) for piece in pieces])

    kept_gains = flat(wide[:, :row_width], narrow, skip_gain_part)
    sent_gains = flat(wide[:, row_width:], narrow, skip_gain_part)
    gain_sums = lax.psum(kept_gains + other_chip(sent_gains), "dp")
    wide_sum = gain_sums[: 3 * row_width].reshape(3, row_width)
    narrow_sum = gain_sums[3 * row_width : 3 * row_width + 4 * HD].reshape(4, HD)
    grad_skip_gain = gain_sums[3 * row_width + 4 * HD :].reshape(2, width)

    def chip_sum(grad, axis):
        size = grad.shape[axis] // 2
        own = lax.slice_in_dim(grad, 0, size, axis=axis)
        sent = lax.slice_in_dim(grad, size, 2 * size, axis=axis).astype(BF16)
        return (own + other_chip(sent).astype(F32)).astype(BF16)

    pieces = [
        chip_sum(grad_down, 1),
        chip_sum(grad_up, 0),
        chip_sum(grad_cross_out, 1),
        chip_sum(grad_cross_query, 0),
        chip_sum(grad_context, 0),
        chip_sum(grad_self_out, 1),
        chip_sum(grad_self_weight, 0),
        chip_sum(grad_skip_weight, 1),
    ]
    totals = []
    for piece in pieces:
        if totals:
            piece = after(piece, totals[-1])
        totals.append(lax.psum(piece, "dp"))
    (
        grad_down,
        grad_up,
        grad_cross_out,
        grad_cross_query,
        grad_context,
        grad_self_out,
        grad_self_weight,
        grad_skip_weight,
    ) = [total.astype(F32) for total in totals]
    return (
        block_out,
        grad_latents,
        grad_skip_input,
        grad_text_states,
        grad_skip_gain,
        grad_skip_weight.reshape(skip_weight.shape),
        grad_shift_weight,
        wide_sum[0],
        grad_self_weight.reshape(self_weight.shape),
        narrow_sum[0],
        narrow_sum[1],
        grad_self_out,
        wide_sum[1],
        grad_cross_query,
        grad_context.reshape(cross_context.shape),
        narrow_sum[2],
        narrow_sum[3],
        grad_cross_out,
        wide_sum[2],
        grad_up,
        grad_down,
    )


def solution(mesh):
    placed = (
        P(("dp", "row"), "col"),
        P(("dp", "row"), "col"),
        P("dp", "col"),
        P(("dp", "col"), "row"),
        P(("dp", "row"), None),
        P(("dp", "col"), "row"),
        P(None, "col"),
        P(None, "col", "row"),
        P("col", "row"),
        P("row"),
        P("row", None, "col"),
        P(),
        P(),
        P("col", "row"),
        P("row"),
        P("row", "col"),
        P("row", None, "col"),
        P(),
        P(),
        P("col", "row"),
        P("row"),
        P("row", "col"),
        P("col", "row"),
    )
    return jax.shard_map(
        shards,
        mesh=mesh,
        in_specs=placed,
        out_specs=(
            P(("dp", "col"), "row"),
            P(("dp", "row"), "col"),
            P(("dp", "row"), "col"),
            P(("dp", "col"), "row"),
            P(None, "col"),
            P(None, "col", "row"),
            P("col", "row"),
            P("row"),
            P("row", None, "col"),
            P(),
            P(),
            P("col", "row"),
            P("row"),
            P("row", "col"),
            P("row", None, "col"),
            P(),
            P(),
            P("col", "row"),
            P("row"),
            P("row", "col"),
            P("col", "row"),
        ),
        check_vma=False,
    )
```

```python
import functools

import jax
import jax.numpy as jnp
from jax import lax
from jax.experimental import pallas as pl
from jax.experimental.pallas import tpu as pltpu
from jax.sharding import PartitionSpec as P

D = 1152
HD = 72
TXT = 333
LAT = 1024


EPSILON = 1e-06
PRECISE = lax.Precision.HIGHEST
SWAP = [(0, 1), (1, 0)]
BF16 = jnp.bfloat16
F32 = jnp.float32
MESH = pl.DeviceIdType.MESH
LOG2E = 1.4426950408889634
FREE = pl.CostEstimate(flops=0, bytes_accessed=0, transcendentals=0)


def other_core(values):
    return lax.ppermute(values, "col", SWAP)


def other_chip(values):
    return lax.ppermute(values, "row", SWAP)


def contract(left_side, right_side):
    return jnp.dot(left_side, right_side, preferred_element_type=F32)


def pair(own):
    return jnp.concatenate([own, other_core(own)])


def after(values, earlier):
    return lax.optimization_barrier((values, earlier))[0]


def dot_nn(a, b):
    return lax.dot_general(a, b, (((1,), (0,)), ((), ())), preferred_element_type=F32)


def dot_tn(a, b):
    return lax.dot_general(a, b, (((0,), (0,)), ((), ())), preferred_element_type=F32)


def dot_nt(a, b):
    return lax.dot_general(a, b, (((1,), (1,)), ((), ())), preferred_element_type=F32)


def lane_norm(values):
    average = jnp.mean(values, axis=0, keepdims=True)
    variance = jnp.mean(values * values, axis=0, keepdims=True) - average * average
    inverse = lax.rsqrt(variance + EPSILON)
    return (values - average) * inverse, inverse


def lane_norm_back(grad, normed, inverse, gain):
    scaled = grad * gain
    first = jnp.mean(scaled, axis=0, keepdims=True)
    second = jnp.mean(scaled * normed, axis=0, keepdims=True)
    return inverse * (scaled - first - normed * second)


def turn(values, cosine, sine):
    quarter = HD // 4
    place = lax.broadcasted_iota(jnp.int32, values.shape, 0)
    leading = (place < quarter) | ((place >= 2 * quarter) & (place < 3 * quarter))
    partner = jnp.where(
        leading,
        pltpu.roll(values, HD - quarter, 0),
        pltpu.roll(values, quarter, 0),
    )
    return values * cosine + partner * sine


def attend_kernel(turned, valid, q_ref, k_ref, v_ref, qg_ref, kg_ref, *rest):
    if turned:
        cos_ref, sin_ref, out_ref, lse_ref = rest
    else:
        out_ref, lse_ref = rest
    query = lane_norm(q_ref[0])[0] * qg_ref[...]
    key = lane_norm(k_ref[0])[0] * kg_ref[...]
    if turned:
        query = turn(query, cos_ref[...], sin_ref[...])
        key = turn(key, cos_ref[...], sin_ref[...])
    query = query.astype(BF16)
    key_rows = key.astype(BF16).T
    value = v_ref[0].astype(BF16)
    keys = value.shape[1]
    ones = jnp.ones((8, keys), BF16)
    if valid < keys:
        ones = jnp.where(lax.broadcasted_iota(jnp.int32, (8, keys), 1) < valid, 1.0, 0.0).astype(BF16)
    tokens = query.shape[1]
    block = 256
    for start in range(0, tokens, block):
        scores = dot_nn(key_rows, query[:, start : start + block])
        weights = jnp.exp2(scores * (LOG2E * HD**-0.5)).astype(BF16)
        total = dot_nn(ones, weights)[:1]
        out = dot_nn(value, weights)
        out_ref[0, :, start : start + block] = (out * (1.0 / total)).astype(BF16)
        lse_ref[0, :, start : start + block] = jnp.log2(total)


def attend_back_kernel(turned, valid, q_ref, k_ref, v_ref, qg_ref, kg_ref, *rest):
    if turned:
        cos_ref, sin_ref, out_ref, lse_ref, grad_ref, grads_ref, gain_ref, dk_acc, dv_acc, dq_acc = rest
    else:
        out_ref, lse_ref, grad_ref, dq_ref, grads_ref, gain_ref, dk_acc, dv_acc, dq_acc = rest
    q_hat, q_inverse = lane_norm(q_ref[0])
    k_hat, k_inverse = lane_norm(k_ref[0])
    query = q_hat * qg_ref[...]
    key = k_hat * kg_ref[...]
    if turned:
        query = turn(query, cos_ref[...], sin_ref[...])
        key = turn(key, cos_ref[...], sin_ref[...])
    query = query.astype(BF16)
    key = key.astype(BF16)
    key_rows = key.T
    value_rows = v_ref[0].astype(BF16).T
    grad = grad_ref[0]
    inner = jnp.sum(grad.astype(F32) * out_ref[0].astype(F32), axis=0, keepdims=True)
    tokens = query.shape[1]
    block = 256
    for start in range(0, tokens, block):
        at = slice(start, start + block)
        scores = dot_nn(key_rows, query[:, at])
        weights = jnp.exp2(scores * (LOG2E * HD**-0.5) - lse_ref[0, :, at])
        grad_weights = dot_nn(value_rows, grad[:, at])
        grad_scores = (weights * (grad_weights - inner[:, at])).astype(BF16)
        weights = weights.astype(BF16)
        dq_acc[:, at] = dot_nn(key, grad_scores)
        grad_value = dot_nt(grad[:, at], weights)
        grad_key = dot_nt(query[:, at], grad_scores)
        if start == 0:
            dk_acc[...] = grad_key
            dv_acc[...] = grad_value
        else:
            dk_acc[...] += grad_key
            dv_acc[...] += grad_value
    grad_query = dq_acc[...] * HD**-0.5
    grad_key = dk_acc[...] * HD**-0.5
    grad_value = dv_acc[...]
    if turned:
        grad_query = turn(grad_query, cos_ref[...], -sin_ref[...])
        grad_key = turn(grad_key, cos_ref[...], -sin_ref[...])
    keys = grad_key.shape[1]
    if valid < keys:
        real = lax.broadcasted_iota(jnp.int32, grad_key.shape, 1) < valid
        grad_key = jnp.where(real, grad_key, 0.0)
        grad_value = jnp.where(real, grad_value, 0.0)
    gain_ref[0, 0] = jnp.sum(grad_query * q_hat, axis=1, keepdims=True)
    gain_ref[0, 1] = jnp.sum(grad_key * k_hat, axis=1, keepdims=True)
    grad_query = lane_norm_back(grad_query, q_hat, q_inverse, qg_ref[...]).astype(BF16)
    grad_key = lane_norm_back(grad_key, k_hat, k_inverse, kg_ref[...]).astype(BF16)
    grads = [grad_key, grad_value.astype(BF16)]
    if turned:
        grads = [grad_query] + grads
    else:
        dq_ref[0] = grad_query
    for index, value in enumerate(grads):
        grads_ref[index, 0] = value


def head_block(array, first):
    return pl.BlockSpec((1,) + array.shape[1:], lambda h: (first + h, 0, 0))


def fixed(array):
    return pl.BlockSpec(array.shape, lambda h: (0,) * array.ndim)


def attend(q, k, v, starts, heads, qg, kg, angles, valid):
    tokens, keys = q.shape[2], k.shape[2]
    extra = list(angles)
    return pl.pallas_call(
        functools.partial(attend_kernel, bool(extra), valid),
        grid=(heads,),
        in_specs=[head_block(q, starts[0]), head_block(k, starts[1]), head_block(v, starts[2])]
        + [fixed(a) for a in [qg, kg] + extra],
        out_specs=[
            pl.BlockSpec((1, HD, tokens), lambda h: (h, 0, 0)),
            pl.BlockSpec((1, 1, tokens), lambda h: (h, 0, 0)),
        ],
        out_shape=[
            jax.ShapeDtypeStruct((heads, HD, tokens), BF16),
            jax.ShapeDtypeStruct((heads, 1, tokens), F32),
        ],
        compiler_params=pltpu.CompilerParams(vmem_limit_bytes=48 * 2**20),
        cost_estimate=FREE,
        name="attend",
    )(q, k, v, qg, kg, *extra)


def attend_back(q, k, v, starts, heads, qg, kg, angles, valid, out, lse, grad):
    tokens, keys = q.shape[2], k.shape[2]
    extra = list(angles)
    parts = 3 if extra else 2
    out_specs = [
        pl.BlockSpec((parts, 1, HD, keys), lambda h: (0, h, 0, 0)),
        pl.BlockSpec((1, 2, HD, 1), lambda h: (h, 0, 0, 0)),
    ]
    out_shape = [
        jax.ShapeDtypeStruct((parts, heads, HD, keys), BF16),
        jax.ShapeDtypeStruct((heads, 2, HD, 1), F32),
    ]
    if not extra:
        out_specs = [pl.BlockSpec((1, HD, tokens), lambda h: (h, 0, 0))] + out_specs
        out_shape = [jax.ShapeDtypeStruct((heads, HD, tokens), BF16)] + out_shape
    return pl.pallas_call(
        functools.partial(attend_back_kernel, bool(extra), valid),
        grid=(heads,),
        in_specs=[head_block(q, starts[0]), head_block(k, starts[1]), head_block(v, starts[2])]
        + [fixed(a) for a in [qg, kg] + extra]
        + [head_block(out, 0), head_block(lse, 0), head_block(grad, 0)],
        out_specs=out_specs,
        out_shape=out_shape,
        scratch_shapes=[
            pltpu.VMEM((HD, keys), F32),
            pltpu.VMEM((HD, keys), F32),
            pltpu.VMEM((HD, tokens), F32),
        ],
        compiler_params=pltpu.CompilerParams(vmem_limit_bytes=48 * 2**20),
        cost_estimate=FREE,
        name="attend_back",
    )(q, k, v, qg, kg, *extra, out, lse, grad)


CHUNK = 256


def core_pair(with_chip=False):
    group, chip, core = (lax.axis_index(axis) for axis in ("dp", "row", "col"))
    other, across = (group, chip, 1 - core), (group, 1 - chip, core)
    barrier = pltpu.get_barrier_semaphore()
    greeted = (other, across) if with_chip else (other,)
    for device in greeted:
        pl.semaphore_signal(barrier, inc=1, device_id=device, device_id_type=MESH)
    pl.semaphore_wait(barrier, len(greeted))
    return (other, across) if with_chip else other


def rows_at(step, base=0):
    return pl.ds(pl.multiple_of(base + step * CHUNK, CHUNK), CHUNK)


def send(src, dst, sems, step, other):
    return pltpu.make_async_remote_copy(
        src_ref=src,
        dst_ref=dst,
        send_sem=sems.at[0, step],
        recv_sem=sems.at[1, step],
        device_id=other,
        device_id_type=MESH,
    )


def join_rows(dst, own, far):
    size = own.shape[0]
    dst[:size] = own[...]
    dst[size:] = far[...]


def join_columns(dst, own, far):
    size = own.shape[1]
    dst[:, :size] = own[...]
    dst[:, size:] = far[...]


def row_norm(values):
    average = jnp.mean(values, axis=1, keepdims=True)
    variance = jnp.mean(values * values, axis=1, keepdims=True) - average * average
    inverse = lax.rsqrt(variance + EPSILON)
    return (values - average) * inverse, inverse


def row_norm_back(grad, normed, inverse, gain):
    scaled = grad * gain
    first = jnp.mean(scaled, axis=1, keepdims=True)
    second = jnp.mean(scaled * normed, axis=1, keepdims=True)
    return inverse * (scaled - first - normed * second)


GELU_A = 0.7978845608028654
GELU_B = 0.044715


def gelu_parts(pre):
    square = pre * pre
    angle = jnp.tanh(GELU_A * pre * (1.0 + GELU_B * square))
    value = 0.5 * pre * (1.0 + angle)
    slope = 0.5 * (1.0 + angle) + 0.5 * pre * (1.0 - angle * angle) * GELU_A * (
        1.0 + 3.0 * GELU_B * square
    )
    return value, slope


def steps(body, half):
    def one(step, carry):
        body(step)
        return carry

    lax.fori_loop(0, half // CHUNK, one, 0)


def forward_kernel(tokens_last, residual, shifted, feed, fetch, *refs):
    refs = list(refs)
    take = lambda: refs.pop(0)
    a_ref, w1o = take(), take()
    w1f = None if fetch else take()
    gain = take()
    res_ref = take() if residual else None
    shift = take() if shifted else None
    w2o = take()
    w2f = None if fetch else take()
    if feed:
        w3o, w3f = take(), take()
    state_ref, x_ref, out_ref = take(), take(), take()
    w1, w2, sent, got, sems, x_sems = take(), take(), take(), take(), take(), take()
    if feed:
        w3, sent_out, got_out, out_sems = take(), take(), take(), take()
    half = state_ref.shape[0]
    if fetch:
        w1f, w2f, far_sems = take(), take(), take()
        other, across = core_pair(True)
        fetches = [
            send(own, far, far_sems, step, across)
            for step, (own, far) in enumerate(((w1o, w1f), (w2o, w2f)))
        ]
        for copy in fetches:
            copy.start()
        fetches[0].wait_recv()
    else:
        other = core_pair()
    join_columns(w1, w1o, w1f)

    def rows_of(step, base):
        if tokens_last:
            return a_ref[:, rows_at(step, base)].T
        return a_ref[rows_at(step, base)]

    def give(step):
        at = rows_at(step)
        sent[at] = dot_nn(rows_of(step, half), w1[...])
        send(sent.at[at], got.at[at], sems, step, other).start()

    steps(give, half)
    if not fetch:
        join_rows(w2, w2o, w2f)
    if feed:
        join_columns(w3, w3o, w3f)

    def keep(step):
        at = rows_at(step)
        state = dot_nn(rows_of(step, 0), w1[...])
        if residual:
            state = state + res_ref[at]
        send(sent.at[at], got.at[at], sems, step, other).wait_recv()
        state = state + got[at]
        state_ref[at] = state
        x = row_norm(state)[0] * gain[...]
        if shifted:
            x = x + shift[...]
        x_ref[at] = x.astype(BF16)
        send(x_ref.at[at], x_ref.at[rows_at(step, half)], x_sems, step, other).start()

    steps(keep, half)
    if fetch:
        fetches[1].wait_recv()
        join_rows(w2, w2o, w2f)

    def arrive(step):
        at = rows_at(step)
        send(x_ref.at[at], x_ref.at[rows_at(step, half)], x_sems, step, other).wait_recv()

    if feed:

        def hidden(step, base):
            pre = dot_nn(x_ref[rows_at(step, base)], w2[...])
            return dot_nn(gelu_parts(pre)[0].astype(BF16), w3[...])

        def give_out(step):
            at = rows_at(step)
            arrive(step)
            sent_out[at] = hidden(step, half)
            send(sent_out.at[at], got_out.at[at], out_sems, step, other).start()

        steps(give_out, half)

        def keep_out(step):
            at = rows_at(step)
            value = hidden(step, 0) + state_ref[at]
            send(sent_out.at[at], got_out.at[at], out_sems, step, other).wait_recv()
            out_ref[at] = (value + got_out[at]).astype(BF16)

        steps(keep_out, half)
    else:

        def near_out(step):
            at = rows_at(step)
            out_ref[:, at] = dot_nn(x_ref[at], w2[...]).T

        steps(near_out, half)

        def far_out(step):
            arrive(step)
            at = rows_at(step, half)
            out_ref[:, at] = dot_nn(x_ref[at], w2[...]).T

        steps(far_out, half)

    def drain(step):
        at = rows_at(step)
        send(sent.at[at], got.at[at], sems, step, other).wait_send()
        send(x_ref.at[at], x_ref.at[rows_at(step, half)], x_sems, step, other).wait_send()
        if feed:
            send(sent_out.at[at], got_out.at[at], out_sems, step, other).wait_send()

    steps(drain, half)
    if fetch:
        for copy in fetches:
            copy.wait_send()


def whole_call(kernel, operands, out_shape, scratch_shapes, collective, name):
    vmem = pl.BlockSpec(memory_space=pltpu.VMEM)
    return pl.pallas_call(
        kernel,
        in_specs=[vmem] * len(operands),
        out_specs=[vmem] * len(out_shape),
        out_shape=[jax.ShapeDtypeStruct(shape, dtype) for shape, dtype in out_shape],
        scratch_shapes=scratch_shapes,
        compiler_params=pltpu.CompilerParams(
            collective_id=collective, has_side_effects=True, vmem_limit_bytes=60 * 2**20
        ),
        cost_estimate=FREE,
        name=name,
    )(*operands)


def pair_sems(half):
    return pltpu.SemaphoreType.DMA((2, half // CHUNK))


def forward_bridge(a, tokens_last, w1, gain, res, shift, w2, w3, collective, name):
    tokens = a.shape[1] if tokens_last else a.shape[0]
    half = tokens // 2
    feed = w3 is not None
    operands = [a, *w1, gain]
    operands += [res] if res is not None else []
    operands += [shift] if shift is not None else []
    operands += [*w2] + ([*w3] if feed else [])
    depth, wide = w1[0].shape[0], w2[0].shape[1]
    out_shape = [((half, D), F32), ((tokens, D), BF16)]
    out_shape += [((half, D), BF16)] if feed else [((wide, tokens), F32)]
    part = pltpu.VMEM((half, D), F32)
    joined = [(depth, D), (D, wide)]
    scratch = [part, part, pair_sems(half), pair_sems(half)]
    if len(w1) == 1:
        out_shape += [(shape, BF16) for shape in joined]
    else:
        scratch = [pltpu.VMEM(shape, BF16) for shape in joined] + scratch
    if feed:
        scratch += [pltpu.VMEM((wide, D), BF16), part, part, pair_sems(half)]
    fetch = len(w1) == 1
    if fetch:
        scratch += [
            pltpu.VMEM(w1[0].shape, BF16),
            pltpu.VMEM(w2[0].shape, BF16),
            pltpu.SemaphoreType.DMA((2, 2)),
        ]
    return whole_call(
        functools.partial(
            forward_kernel, tokens_last, res is not None, shift is not None, feed, fetch
        ),
        operands,
        out_shape,
        scratch,
        collective,
        name,
    )


def backward_kernel(feed, summed, tokens_last, whole, *refs):
    refs = list(refs)
    take = lambda: refs.pop(0)
    if feed:
        cot_ref, feed_ref, w3o, w3f = take(), take(), take(), take()
    else:
        g_ref, res_ref = take(), take()
    if whole:
        w2, state_ref, gain, w1 = take(), take(), take(), take()
    else:
        w2o, w2f, state_ref, gain, w1o, w1f = (take() for _ in range(6))
    if feed:
        hidden_ref, pre_ref = take(), take()
    total_ref, b_ref, out_ref, gain_ref = take(), take(), take(), take()
    if summed:
        sum_ref = take()
    if not whole:
        w1, w2 = take(), take()
    sent, got, sems, x_sems = take(), take(), take(), take()
    if feed:
        w3 = take()
    half = state_ref.shape[0]
    other = core_pair()
    if not whole:
        join_rows(w2, w2o, w2f)
    if feed:
        join_columns(w3, w3o, w3f)

    def part(step, base):
        at = rows_at(step, base)
        if feed:
            value, slope = gelu_parts(dot_nn(feed_ref[at], w2[...]))
            hidden_ref[at] = value.astype(BF16)
            rows = (dot_nt(cot_ref[at], w3[...]) * slope).astype(BF16)
            pre_ref[at] = rows
        else:
            rows = g_ref[:, at].T
        return dot_nt(rows, w2[...])

    def give(step):
        at = rows_at(step)
        sent[at] = part(step, half)
        send(sent.at[at], got.at[at], sems, step, other).start()

    steps(give, half)
    if not whole:
        join_columns(w1, w1o, w1f)
    gain_ref[...] = jnp.zeros_like(gain_ref)
    if summed:
        sum_ref[...] = jnp.zeros_like(sum_ref)

    def keep(step):
        at = rows_at(step)
        grad = part(step, 0)
        send(sent.at[at], got.at[at], sems, step, other).wait_recv()
        grad = grad + got[at]
        normed, inverse = row_norm(state_ref[at])
        gain_ref[...] += jnp.sum(grad * normed, axis=0, keepdims=True)
        if summed:
            sum_ref[...] += jnp.sum(grad, axis=0, keepdims=True)
        back = row_norm_back(grad, normed, inverse, gain[...])
        total = back + (cot_ref[at].astype(F32) if feed else res_ref[at])
        total_ref[at] = total
        b_ref[at] = total.astype(BF16)
        send(b_ref.at[at], b_ref.at[rows_at(step, half)], x_sems, step, other).start()

    steps(keep, half)

    def product(at):
        value = dot_nt(b_ref[at], w1[...])
        if tokens_last:
            out_ref[:, at] = value.T.astype(out_ref.dtype)
        else:
            out_ref[at] = value.astype(out_ref.dtype)

    def near_out(step):
        product(rows_at(step))

    steps(near_out, half)

    def far_out(step):
        at = rows_at(step)
        send(b_ref.at[at], b_ref.at[rows_at(step, half)], x_sems, step, other).wait_recv()
        product(rows_at(step, half))

    steps(far_out, half)

    def drain(step):
        at = rows_at(step)
        send(sent.at[at], got.at[at], sems, step, other).wait_send()
        send(b_ref.at[at], b_ref.at[rows_at(step, half)], x_sems, step, other).wait_send()

    steps(drain, half)


def backward_bridge(g, res, feed, w2, state, gain, w1, summed, tokens_last, collective, name):
    half = state.shape[0]
    tokens = 2 * half
    depth, wide = w2[0].shape[1], w1[0].shape[0]
    if feed:
        operands = [feed[0], feed[1], *feed[2]]
    else:
        operands = [g, res]
    operands += [*w2, state, gain, *w1]
    out_shape = [((tokens, depth), BF16)] * 2 if feed else []
    out_shape += [((half, D), F32), ((tokens, D), BF16)]
    out_shape += [((wide, tokens), BF16)] if tokens_last else [((tokens, wide), F32)]
    out_shape += [((1, D), F32)] * (2 if summed else 1)
    part = pltpu.VMEM((half, D), F32)
    scratch = [part, part, pair_sems(half), pair_sems(half)]
    whole = len(w1) == 1
    if not whole:
        scratch = [pltpu.VMEM((wide, D), BF16), pltpu.VMEM((D, depth), BF16)] + scratch
    if feed:
        scratch += [pltpu.VMEM((depth, D), BF16)]
    return whole_call(
        functools.partial(backward_kernel, bool(feed), summed, tokens_last, whole),
        operands,
        out_shape,
        scratch,
        collective,
        name,
    )


def product_kernel(by_rows, left_last, left_ref, right_ref, own_ref, far_ref):
    left, right = left_ref[...], right_ref[...]
    if by_rows:
        if left_last:
            value = dot_nn(left, right).T
        else:
            value = dot_tn(right, left)
        value = value.astype(BF16)
        size = value.shape[0] // 2
        parts = (value[:size], value[size:])
    else:
        value = dot_nn(left, right) if left_last else dot_tn(left, right)
        value = value.astype(BF16)
        size = value.shape[1] // 2
        parts = (value[:, :size], value[:, size:])
    for part, ref in zip(parts, (own_ref, far_ref)):
        rows, columns = ref.shape
        if part.shape == ref.shape:
            ref[...] = part
        else:
            ref[:, : columns // 2] = part[:rows]
            ref[:, columns // 2 :] = part[rows:]


def weight_product(left, left_last, right, by_rows, tile, name):
    wide = left.shape[0] if left_last else left.shape[1]
    tokens, across = right.shape
    if left_last:
        left_spec = pl.BlockSpec((tile, tokens), lambda i: (i, 0))
    else:
        left_spec = pl.BlockSpec((tokens, tile), lambda i: (0, i))
    rows = tile * across // 2 // D
    out_spec = pl.BlockSpec((rows, D), lambda i: (i, 0))
    out_shape = jax.ShapeDtypeStruct((rows * (wide // tile), D), BF16)
    return pl.pallas_call(
        functools.partial(product_kernel, by_rows, left_last),
        grid=(wide // tile,),
        in_specs=[left_spec, pl.BlockSpec((tokens, across), lambda i: (0, 0))],
        out_specs=[out_spec, out_spec],
        out_shape=[out_shape, out_shape],
        compiler_params=pltpu.CompilerParams(vmem_limit_bytes=48 * 2**20),
        cost_estimate=FREE,
        name=name,
    )(left, right)


def pieces_of(rows):
    for pieces in (3, 2, 5):
        if rows % (16 * pieces) == 0:
            return pieces
    return 1


def ring_kernel(size, plan, *refs):
    refs = list(refs)
    sections = len(plan)

    def take(count):
        return [refs.pop(0) for _ in range(count)]

    own_refs = [take(len(parts)) for _, parts in plan]
    far_refs = [take(len(parts)) for _, parts in plan]
    out_refs = take(sections)
    work_refs = take(sections)
    slot_refs = take(sections)
    sends, arrivals, far_sems = take(3)
    index = lax.axis_index("dp")
    chip = lax.axis_index("row")
    core = lax.axis_index("col")
    across = size // 2
    side = lax.rem(index, 2)
    level = index // 2
    place = (1 - side) * level + side * (size - 1 - level)

    def device_at(where):
        where = lax.rem(where + size, size)
        turned = where // across
        high = (1 - turned) * where + turned * (size - 1 - where)
        return (high * 2 + turned, chip, core)

    neighbours = (device_at(place + 1), device_at(place - 1))
    partner = (index, 1 - chip, core)
    barrier = pltpu.get_barrier_semaphore()
    for device in neighbours + (partner,):
        pl.semaphore_signal(barrier, inc=1, device_id=device, device_id_type=MESH)
    pl.semaphore_wait(barrier, 3)

    exchanges = []
    for section in range(sections):
        exchanges.append([])
        if plan[section][0]:
            base = 0
            for number, far in enumerate(far_refs[section]):
                rows = far.shape[0]
                exchange = pltpu.make_async_remote_copy(
                    src_ref=far,
                    dst_ref=work_refs[section].at[base : base + rows],
                    send_sem=far_sems.at[0, section, number],
                    recv_sem=far_sems.at[1, section, number],
                    device_id=partner,
                    device_id_type=MESH,
                )
                exchange.start()
                exchanges[section].append(exchange)
                base += rows

    def ring(which, source, total, slots):
        half = source.shape[0] // 2
        rows = half // size
        pieces = pieces_of(rows)
        piece = rows // pieces

        def span(way, chunk, part):
            chunk = lax.rem(chunk + 2 * size, size)
            return pl.ds(pl.multiple_of(way * half + chunk * rows + part * piece, 16), piece)

        def chunk_of(way, step):
            return place - step if way == 0 else place + step

        def within(part):
            return pl.ds(part * piece, piece)

        def copy(way, part, step, src, dst, phase):
            return pltpu.make_async_remote_copy(
                src_ref=src,
                dst_ref=dst,
                send_sem=sends.at[which, phase, way, part, step],
                recv_sem=arrivals.at[which, phase, way, part, step],
                device_id=neighbours[way],
                device_id_type=MESH,
            )

        def first(way, part):
            src = source.at[span(way, chunk_of(way, 0), part)]
            return copy(way, part, 0, src, slots.at[way, 0, within(part)], 0)

        def reduced(way, part, step):
            src = slots.at[way, step - 1, within(part)]
            return copy(way, part, step, src, slots.at[way, step, within(part)], 0)

        def spread(way, part, step):
            at = span(way, chunk_of(way, step) + (1 if way == 0 else -1), part)
            return copy(way, part, step, total.at[at], total.at[at], 1)

        def arrival(way, part, step):
            return first(way, part) if isinstance(step, int) else reduced(way, part, step)

        def added(way, part, step):
            at = span(way, chunk_of(way, step + 1), part)
            got = slots[way, step, within(part)]
            return at, (source[at].astype(F32) + got.astype(F32)).astype(BF16)

        each = [(way, part) for part in range(pieces) for way in range(2)]
        for way, part in each:
            first(way, part).start()

        def reduce_step(step, carry):
            for way, part in each:
                arrival(way, part, step).wait_recv()
                _, value = added(way, part, step)
                slots[way, step, within(part)] = value
                reduced(way, part, step + 1).start()
            return carry

        reduce_step(0, 0)
        lax.fori_loop(1, size - 2, reduce_step, 0)
        for way, part in each:
            reduced(way, part, size - 2).wait_recv()
            at, value = added(way, part, size - 2)
            total[at] = value
            spread(way, part, 0).start()

        def gather_step(step, carry):
            for way, part in each:
                spread(way, part, step).wait_recv()
                spread(way, part, step + 1).start()
            return carry

        lax.fori_loop(0, size - 2, gather_step, 0)
        for way, part in each:
            spread(way, part, size - 2).wait_recv()
            first(way, part).wait_send()
            spread(way, part, 0).wait_send()

        def drain(step, carry):
            for way, part in each:
                reduced(way, part, step).wait_send()
                spread(way, part, step).wait_send()
            return carry

        lax.fori_loop(1, size - 1, drain, 0)

    for section in range(sections):
        exchanged, parts = plan[section]
        work = work_refs[section]
        base = 0
        for number, rows in enumerate(parts):
            own = own_refs[section][number][...]
            if exchanged:
                exchanges[section][number].wait()
                near = work[base : base + rows]
            else:
                near = far_refs[section][number][...]
            work[base : base + rows] = (own.astype(F32) + near.astype(F32)).astype(BF16)
            base += rows
        if base < work.shape[0]:
            work[base:] = jnp.zeros((work.shape[0] - base, work.shape[1]), BF16)
        ring(section, work, out_refs[section], slot_refs[section])


def ring_sum(size, sections):
    vmem = pl.BlockSpec(memory_space=pltpu.VMEM)
    plan = tuple((exchanged, tuple(own.shape[0] for own in owns)) for exchanged, owns, _ in sections)
    owns = [own for _, parts, _ in sections for own in parts]
    fars = [far for _, _, parts in sections for far in parts]
    totals = [sum(parts) for _, parts in plan]
    totals = [rows + -rows % (32 * size) for rows in totals]
    whole = [pltpu.VMEM((rows, D), BF16) for rows in totals]
    slots = [pltpu.VMEM((2, size - 1, rows // 2 // size, D), BF16) for rows in totals]
    pieces = max(pieces_of(rows // 2 // size) for rows in totals)
    sems = pltpu.SemaphoreType.DMA((len(sections), 2, 2, pieces, size - 1))
    most = max(len(parts) for _, parts in plan)
    return pl.pallas_call(
        functools.partial(ring_kernel, size, plan),
        in_specs=[vmem] * (len(owns) + len(fars)),
        out_specs=[vmem] * len(sections),
        out_shape=[jax.ShapeDtypeStruct((rows, D), BF16) for rows in totals],
        scratch_shapes=whole
        + slots
        + [sems, sems, pltpu.SemaphoreType.DMA((2, len(sections), most))],
        compiler_params=pltpu.CompilerParams(
            collective_id=0, has_side_effects=True, vmem_limit_bytes=62 * 2**20
        ),
        cost_estimate=FREE,
        name="ring_sum",
    )(*owns, *fars)


def shards(
    latents,
    skip_input,
    condition,
    text_states,
    positions,
    cotangent,
    skip_gain,
    skip_weight,
    shift_weight,
    self_gain,
    self_weight,
    query_gain,
    key_gain,
    self_out,
    cross_gain,
    cross_query,
    cross_context,
    cross_query_gain,
    cross_key_gain,
    cross_out,
    feed_gain,
    up_weight,
    down_weight,
):
    tokens, width = latents.shape
    half = tokens // 2
    heads_here = width // HD
    core = lax.axis_index("col")
    chip = lax.axis_index("row")
    straight = core == chip

    def own_first(values):
        return (
            lax.dynamic_slice_in_dim(values, core * half, half, 0),
            lax.dynamic_slice_in_dim(values, (1 - core) * half, half, 0),
        )

    def in_order(own, other):
        return jnp.where(
            core == 0, jnp.concatenate([own, other]), jnp.concatenate([other, own])
        )

    skip_flat = skip_weight.reshape(2 * width, -1)
    self_flat = self_weight.reshape(-1, 3 * width)
    context_flat = cross_context.reshape(-1, 2 * width)

    rows = up_weight.shape[0]
    norm_far = other_chip(jnp.stack([self_gain, cross_gain, feed_gain]))

    def near_and_far(weight):
        return (weight, other_chip(weight))

    def share_of(weight):
        share = weight.shape[0] // lax.axis_size("dp")
        piece = lax.dynamic_slice_in_dim(weight, lax.axis_index("dp") * share, share, 0)
        return other_chip(piece)

    up_share, down_share = share_of(up_weight), share_of(down_weight)
    up_pair = (up_weight, lax.all_gather(up_share, "dp", axis=0, tiled=True))
    down_pair = (down_weight, lax.all_gather(down_share, "dp", axis=0, tiled=True))
    norm_gains = jnp.concatenate([jnp.stack([self_gain, cross_gain, feed_gain]), norm_far], axis=1)
    self_gain_all, cross_gain_all, feed_gain_all = norm_gains[0:1], norm_gains[1:2], norm_gains[2:3]

    text_near = other_core(text_states)
    text_mine = jnp.where(straight, text_states, text_near)
    text_here = text_states.shape[0]
    kept, handed = own_first(cotangent)
    handed = other_core(handed)
    cot_mine = jnp.where(straight, kept, handed)

    place_own, place_other = own_first(positions)
    places = jnp.concatenate([place_own, place_other]).astype(F32)
    quarter = HD // 4
    frequency = 10000.0 ** (-jnp.arange(quarter, dtype=F32) / quarter)
    angles = frequency[:, None] * places.T[:, None, :]
    cosine = jnp.cos(angles)
    sine = jnp.sin(angles)
    cosine = jnp.stack([cosine, cosine], axis=1).reshape(HD, tokens)
    sine = jnp.stack([-sine, sine], axis=1).reshape(HD, tokens)

    lat_own, lat_other = own_first(latents)
    skip_own, skip_other = own_first(skip_input)
    lat = jnp.concatenate([lat_own, lat_other]).astype(F32)
    joint = jnp.concatenate([skip_own, skip_other]).astype(F32)
    sums = jnp.stack(
        [jnp.sum(lat, axis=1) + jnp.sum(joint, axis=1), jnp.sum(lat * lat, axis=1) + jnp.sum(joint * joint, axis=1)]
    )

    def swap_halves(values):
        return jnp.concatenate([values[:, half:], values[:, :half]], axis=1)

    sums = sums + swap_halves(other_core(sums))
    average = (sums[0] / (2 * D))[:, None]
    skip_inverse = lax.rsqrt((sums[1] / (2 * D))[:, None] - average * average + EPSILON)
    skip_low = jnp.concatenate(
        [
            (lat - average) * skip_inverse * skip_gain[0],
            (joint - average) * skip_inverse * skip_gain[1],
        ],
        axis=1,
    ).astype(BF16)

    cond_low = jax.nn.silu(condition.astype(F32)).astype(BF16)
    shift_part = contract(cond_low, shift_weight)
    shift_part = shift_part + other_core(shift_part)
    shift_mine = lax.dynamic_slice_in_dim(shift_part, chip, 1, 0)
    shift_far = other_chip(lax.dynamic_slice_in_dim(shift_part, 1 - chip, 1, 0))
    shift_row = jnp.concatenate([shift_mine, shift_far], axis=1)

    first_state, first_all, mixed_raw, skip_whole, self_whole = forward_bridge(
        skip_low, False, (skip_flat,), self_gain_all, None, shift_row, (self_flat,), None, 1, "into_self"
    )
    mixed_raw = mixed_raw.reshape(3 * heads_here, HD, tokens)

    def near_and_later(weight):
        return (weight, other_chip(after(weight, first_all)))

    out_pair = near_and_later(self_out)
    query_pair = near_and_later(cross_query)
    text_far = other_chip(after(jnp.where(straight, text_near, text_states), first_all))
    context_pair = near_and_later(context_flat)
    context_far = context_pair[1]
    cross_pair = near_and_later(cross_out)
    cot_far = other_chip(after(jnp.where(straight, handed, kept), context_far))
    text_all = jnp.concatenate([text_mine, text_far], axis=1)
    text_all = jnp.pad(text_all, ((0, -text_here % 128), (0, 0)))
    context_all = jnp.concatenate([context_flat, context_far])
    self_args = (
        (mixed_raw, mixed_raw, mixed_raw),
        (0, heads_here, 2 * heads_here),
        heads_here,
        query_gain[:, None],
        key_gain[:, None],
        (cosine, sine),
        tokens,
    )
    heads_low, log_first = attend(*self_args[0], *self_args[1:])
    heads_flat = heads_low.reshape(width, tokens)
    second_state, cross_all, probe_raw = forward_bridge(
        heads_flat, True, out_pair, cross_gain_all, first_state, None, query_pair, None, 2, "into_cross"
    )
    probe_raw = probe_raw.reshape(heads_here, HD, tokens)
    memory_raw = lax.dot_general(
        context_all, text_all, (((0,), (1,)), ((), ())), preferred_element_type=F32
    ).reshape(2 * heads_here, HD, -1)
    cross_args = (
        (probe_raw, memory_raw, memory_raw),
        (0, 0, heads_here),
        heads_here,
        cross_query_gain[:, None],
        cross_key_gain[:, None],
        (),
        text_here,
    )
    cross_low, log_second = attend(*cross_args[0], *cross_args[1:])
    cross_flat = cross_low.reshape(width, tokens)
    third_state, feed_all, out_own = forward_bridge(
        cross_flat, True, cross_pair, feed_gain_all, second_state, None, up_pair, down_pair, 3, "into_feed"
    )
    row_width = up_weight.shape[0]
    out_mine = out_own[:, :row_width]
    out_far = other_chip(out_own[:, row_width:])

    cot_own = jnp.concatenate([cot_mine, after(cot_far, cross_all)], axis=1)
    cot_all = pair(cot_own)
    (
        hidden_low,
        grad_pre,
        grad_third,
        branch_two_all,
        grad_cross_heads,
        feed_gain_part,
    ) = backward_bridge(
        None,
        None,
        (cot_all, feed_all, down_pair),
        up_pair,
        third_state,
        feed_gain_all,
        cross_pair,
        False,
        True,
        4,
        "from_feed",
    )
    down_own, down_far = weight_product(hidden_low, False, cot_all, False, 768, "grad_down")
    up_own, up_far = weight_product(grad_pre, False, feed_all, True, 1152, "grad_up")
    cross_own, cross_far = weight_product(
        cross_flat, True, branch_two_all, False, 576, "grad_cross_out"
    )
    down_far_here = other_chip(down_far)
    up_far_here = other_chip(up_far)
    grad_cross_heads = after(grad_cross_heads, (down_far, up_far))
    grad_probe, grad_memory, grad_cross_gains = attend_back(
        *cross_args[0],
        *cross_args[1:],
        cross_low,
        log_second,
        grad_cross_heads.reshape(heads_here, HD, tokens),
    )
    probe_low = grad_probe.reshape(width, tokens)
    query_own, query_far = weight_product(probe_low, True, cross_all, True, 576, "grad_cross_query")
    memory_low = grad_memory.reshape(2 * width, -1)
    context_own, context_far = weight_product(
        memory_low, True, text_all, True, 576, "grad_context"
    )
    text_part = lax.dot_general(
        memory_low, context_all, (((0,), (1,)), ((), ())), preferred_element_type=F32
    )[:text_here]
    text_width = text_states.shape[1]
    text_one, text_two = text_part[:, :text_width], text_part[:, text_width:]
    text_sum = jnp.where(straight, text_one, text_two) + other_core(
        jnp.where(straight, text_two, text_one)
    )
    text_sum = text_sum.astype(BF16)
    text_back = lax.ppermute(text_sum, ("row", "col"), [(1, 2), (2, 1)])
    grad_text_states = jnp.where(straight, text_sum, text_back)

    grad_second, branch_one_all, grad_heads, cross_gain_part = backward_bridge(
        probe_low,
        grad_third,
        None,
        query_pair,
        second_state,
        cross_gain_all,
        out_pair,
        False,
        True,
        5,
        "from_cross",
    )
    out_grad_own, out_grad_far = weight_product(
        heads_flat, True, branch_one_all, False, 576, "grad_self_out"
    )
    grad_heads_in = after(grad_heads, down_far_here)
    grad_mixed, grad_self_gains = attend_back(
        *self_args[0],
        *self_args[1:],
        heads_low,
        log_first,
        grad_heads_in.reshape(heads_here, HD, tokens),
    )
    mixed_low = grad_mixed.reshape(3 * width, tokens)
    self_own, self_far = weight_product(mixed_low, True, first_all, True, 576, "grad_self")
    _, grad_first_all, grad_skip_out, self_gain_part, shift_grad = backward_bridge(
        mixed_low,
        grad_second,
        None,
        (self_whole,),
        first_state,
        self_gain_all,
        (skip_whole,),
        True,
        False,
        6,
        "from_self",
    )
    skip_own, skip_far = weight_product(skip_low, False, grad_first_all, False, 384, "grad_skip")
    shift_grad = shift_grad + other_core(shift_grad)
    shift_here = shift_grad[:, :row_width]
    shift_there = other_chip(shift_grad[:, row_width:])
    shift_pair = jnp.where(
        chip == 0,
        jnp.concatenate([shift_here, shift_there]),
        jnp.concatenate([shift_there, shift_here]),
    )
    out_far = after(out_far, grad_skip_out)
    out_kept = jnp.where(straight, out_mine, out_far)
    out_got = other_core(jnp.where(straight, out_far, out_mine))
    block_out = in_order(out_kept, out_got)
    lat_normed = (lat - average) * skip_inverse
    joint_normed = (joint - average) * skip_inverse
    grad_lat, grad_joint = grad_skip_out[:, :width], grad_skip_out[:, width:]
    lat_scaled, joint_scaled = grad_lat * skip_gain[0], grad_joint * skip_gain[1]
    sums_back = jnp.stack(
        [
            jnp.sum(lat_scaled, axis=1) + jnp.sum(joint_scaled, axis=1),
            jnp.sum(lat_scaled * lat_normed, axis=1) + jnp.sum(joint_scaled * joint_normed, axis=1),
        ]
    )
    sums_back = sums_back + swap_halves(other_core(sums_back))
    first_mean = (sums_back[0] / (2 * D))[:, None]
    second_mean = (sums_back[1] / (2 * D))[:, None]
    skip_gain_part = jnp.stack(
        [jnp.sum(grad_lat * lat_normed, axis=0), jnp.sum(grad_joint * joint_normed, axis=0)]
    )
    grad_lat = (skip_inverse * (lat_scaled - first_mean - lat_normed * second_mean)).astype(BF16)
    grad_joint = (skip_inverse * (joint_scaled - first_mean - joint_normed * second_mean)).astype(BF16)
    grad_latents = in_order(grad_lat[:half], grad_lat[half:])
    grad_skip_input = in_order(grad_joint[:half], grad_joint[half:])

    wide = jnp.concatenate([self_gain_part, cross_gain_part, feed_gain_part])
    wide = wide + other_core(wide)
    narrow = jnp.concatenate([jnp.sum(grad_self_gains, axis=0), jnp.sum(grad_cross_gains, axis=0)])
    narrow = narrow[:, :, 0]
    narrow = narrow + other_core(narrow)

    def flat(*pieces):
        return jnp.concatenate([piece.reshape(-1) for piece in pieces])

    kept_gains = flat(wide[:, :row_width], narrow, skip_gain_part)
    sent_gains = flat(wide[:, row_width:], narrow, skip_gain_part)
    small = flat(
        kept_gains + other_chip(sent_gains), cond_low.astype(F32), shift_pair
    )
    groups = lax.axis_size("dp")
    smalls = [small] + [
        lax.ppermute(small, "dp", [(i, (i + k) % groups) for i in range(groups)])
        for k in range(1, groups)
    ]
    down_sum = (down_own.astype(F32) + down_far_here.astype(F32)).astype(BF16)
    up_far_here = after(up_far_here, down_sum)
    high, middle, inner, last = ring_sum(
        groups,
        [
            (False, [up_own], [up_far_here]),
            (
                True,
                [cross_own, out_grad_own, query_own, context_own],
                [cross_far, out_grad_far, query_far, context_far],
            ),
            (True, [self_own], [self_far]),
            (True, [skip_own], [skip_far]),
        ],
    )
    grad_down = lax.psum(down_sum, "dp")

    def unpack(block, count):
        rows = block.shape[0] // count
        pieces = [block[i * rows : (i + 1) * rows] for i in range(count)]
        return [
            jnp.concatenate([piece[:, :width], piece[:, width:]]).astype(F32) for piece in pieces
        ]

    grad_down = jnp.concatenate(unpack(grad_down, 3))
    grad_up = jnp.concatenate([high[:row_width], high[row_width : 2 * row_width]], axis=1)
    grad_up = grad_up.astype(F32)
    place = width // 2
    grad_cross_out, grad_self_out, grad_cross_query = unpack(middle[: 3 * place], 3)
    grad_context = unpack(middle[3 * place : 3 * place + text_width], 2)
    grad_context = jnp.concatenate([grad_context[0], grad_context[1]], axis=1)
    grad_self_weight = jnp.stack(unpack(inner[: 3 * place], 3), axis=1)
    grad_skip_weight = jnp.concatenate(unpack(last[: 2 * place], 3))

    smalls = [after(value, last) for value in smalls[1:]] + smalls[:1]
    gain_count = kept_gains.shape[0]
    gain_sums = sum(value[:gain_count] for value in smalls)
    images = condition.shape[0]
    conds = [
        value[gain_count : gain_count + images * width].reshape(images, width) for value in smalls
    ]
    shifts = [value[gain_count + images * width :].reshape(images, row_width) for value in smalls]
    grad_shift_weight = lax.dot_general(
        jnp.concatenate(conds),
        jnp.concatenate(shifts),
        (((0,), (0,)), ((), ())),
        precision=PRECISE,
        preferred_element_type=F32,
    )
    wide_sum = gain_sums[: 3 * row_width].reshape(3, row_width)
    narrow_sum = gain_sums[3 * row_width : 3 * row_width + 4 * HD].reshape(4, HD)
    grad_skip_gain = gain_sums[3 * row_width + 4 * HD :].reshape(2, width)

    return (
        block_out,
        grad_latents,
        grad_skip_input,
        grad_text_states,
        grad_skip_gain,
        grad_skip_weight.reshape(skip_weight.shape),
        grad_shift_weight,
        wide_sum[0],
        grad_self_weight.reshape(self_weight.shape),
        narrow_sum[0],
        narrow_sum[1],
        grad_self_out,
        wide_sum[1],
        grad_cross_query,
        grad_context.reshape(cross_context.shape),
        narrow_sum[2],
        narrow_sum[3],
        grad_cross_out,
        wide_sum[2],
        grad_up,
        grad_down,
    )


def solution(mesh):
    placed = (
        P(("dp", "row"), "col"),
        P(("dp", "row"), "col"),
        P("dp", "col"),
        P(("dp", "col"), "row"),
        P(("dp", "row"), None),
        P(("dp", "col"), "row"),
        P(None, "col"),
        P(None, "col", "row"),
        P("col", "row"),
        P("row"),
        P("row", None, "col"),
        P(),
        P(),
        P("col", "row"),
        P("row"),
        P("row", "col"),
        P("row", None, "col"),
        P(),
        P(),
        P("col", "row"),
        P("row"),
        P("row", "col"),
        P("col", "row"),
    )
    return jax.shard_map(
        shards,
        mesh=mesh,
        in_specs=placed,
        out_specs=(
            P(("dp", "col"), "row"),
            P(("dp", "row"), "col"),
            P(("dp", "row"), "col"),
            P(("dp", "col"), "row"),
            P(None, "col"),
            P(None, "col", "row"),
            P("col", "row"),
            P("row"),
            P("row", None, "col"),
            P(),
            P(),
            P("col", "row"),
            P("row"),
            P("row", "col"),
            P("row", None, "col"),
            P(),
            P(),
            P("col", "row"),
            P("row"),
            P("row", "col"),
            P("col", "row"),
        ),
        check_vma=False,
    )
```

```python
import functools

import jax
import jax.numpy as jnp
from jax import lax
from jax.experimental import pallas as pl
from jax.experimental.pallas import tpu as pltpu
from jax.sharding import PartitionSpec as P

D = 1152
HD = 72
TXT = 333
LAT = 1024


EPSILON = 1e-06
PRECISE = lax.Precision.HIGHEST
SWAP = [(0, 1), (1, 0)]
BF16 = jnp.bfloat16
F32 = jnp.float32
MESH = pl.DeviceIdType.MESH
LOG2E = 1.4426950408889634
TIMES = {
    "attend": 15,
    "attend_cross": 7,
    "attend_back": 29,
    "attend_back_cross": 16,
    "into_self": 90,
    "into_cross": 15,
    "into_feed": 28,
    "from_feed": 40,
    "from_cross": 16,
    "from_self": 22,
    "grad_down": 9,
    "grad_up": 9,
    "grad_cross_out": 3,
    "grad_cross_query": 3,
    "grad_context": 3,
    "grad_self_out": 3,
    "grad_self": 8,
    "grad_skip": 6,
    "ring_sum": 200,
}
SHARE = 3.0


def cost(name):
    return pl.CostEstimate(
        flops=0, bytes_accessed=int(TIMES[name] * 3.69e6 / SHARE), transcendentals=0
    )


def other_core(values):
    return lax.ppermute(values, "col", SWAP)


def other_chip(values):
    return lax.ppermute(values, "row", SWAP)


def contract(left_side, right_side):
    return jnp.dot(left_side, right_side, preferred_element_type=F32)


def pair(own):
    return jnp.concatenate([own, other_core(own)])


def after(values, earlier):
    return lax.optimization_barrier((values, earlier))[0]


def dot_nn(a, b):
    return lax.dot_general(a, b, (((1,), (0,)), ((), ())), preferred_element_type=F32)


def dot_tn(a, b):
    return lax.dot_general(a, b, (((0,), (0,)), ((), ())), preferred_element_type=F32)


def dot_nt(a, b):
    return lax.dot_general(a, b, (((1,), (1,)), ((), ())), preferred_element_type=F32)


def lane_norm(values):
    average = jnp.mean(values, axis=0, keepdims=True)
    variance = jnp.mean(values * values, axis=0, keepdims=True) - average * average
    inverse = lax.rsqrt(variance + EPSILON)
    return (values - average) * inverse, inverse


def lane_norm_back(grad, normed, inverse, gain):
    scaled = grad * gain
    first = jnp.mean(scaled, axis=0, keepdims=True)
    second = jnp.mean(scaled * normed, axis=0, keepdims=True)
    return inverse * (scaled - first - normed * second)


def turn(values, cosine, sine):
    quarter = HD // 4
    place = lax.broadcasted_iota(jnp.int32, values.shape, 0)
    leading = (place < quarter) | ((place >= 2 * quarter) & (place < 3 * quarter))
    partner = jnp.where(
        leading,
        pltpu.roll(values, HD - quarter, 0),
        pltpu.roll(values, quarter, 0),
    )
    return values * cosine + partner * sine


def attend_kernel(turned, valid, q_ref, k_ref, v_ref, qg_ref, kg_ref, *rest):
    if turned:
        cos_ref, sin_ref, out_ref, lse_ref = rest
    else:
        out_ref, lse_ref = rest
    query = lane_norm(q_ref[0])[0] * qg_ref[...]
    key = lane_norm(k_ref[0])[0] * kg_ref[...]
    if turned:
        query = turn(query, cos_ref[...], sin_ref[...])
        key = turn(key, cos_ref[...], sin_ref[...])
    query = query.astype(BF16)
    key_rows = key.astype(BF16).T
    value = v_ref[0].astype(BF16)
    keys = value.shape[1]
    ones = jnp.ones((8, keys), BF16)
    if valid < keys:
        ones = jnp.where(lax.broadcasted_iota(jnp.int32, (8, keys), 1) < valid, 1.0, 0.0).astype(BF16)
    tokens = query.shape[1]
    block = 256
    for start in range(0, tokens, block):
        scores = dot_nn(key_rows, query[:, start : start + block])
        weights = jnp.exp2(scores * (LOG2E * HD**-0.5)).astype(BF16)
        total = dot_nn(ones, weights)[:1]
        out = dot_nn(value, weights)
        out_ref[0, :, start : start + block] = (out * (1.0 / total)).astype(BF16)
        lse_ref[0, :, start : start + block] = jnp.log2(total)


def attend_back_kernel(turned, valid, q_ref, k_ref, v_ref, qg_ref, kg_ref, *rest):
    if turned:
        cos_ref, sin_ref, out_ref, lse_ref, grad_ref, grads_ref, gain_ref, dk_acc, dv_acc, dq_acc = rest
    else:
        out_ref, lse_ref, grad_ref, dq_ref, grads_ref, gain_ref, dk_acc, dv_acc, dq_acc = rest
    q_hat, q_inverse = lane_norm(q_ref[0])
    k_hat, k_inverse = lane_norm(k_ref[0])
    query = q_hat * qg_ref[...]
    key = k_hat * kg_ref[...]
    if turned:
        query = turn(query, cos_ref[...], sin_ref[...])
        key = turn(key, cos_ref[...], sin_ref[...])
    query = query.astype(BF16)
    key = key.astype(BF16)
    key_rows = key.T
    value_rows = v_ref[0].astype(BF16).T
    grad = grad_ref[0]
    inner = jnp.sum(grad.astype(F32) * out_ref[0].astype(F32), axis=0, keepdims=True)
    tokens = query.shape[1]
    block = 256
    for start in range(0, tokens, block):
        at = slice(start, start + block)
        scores = dot_nn(key_rows, query[:, at])
        weights = jnp.exp2(scores * (LOG2E * HD**-0.5) - lse_ref[0, :, at])
        grad_weights = dot_nn(value_rows, grad[:, at])
        grad_scores = (weights * (grad_weights - inner[:, at])).astype(BF16)
        weights = weights.astype(BF16)
        dq_acc[:, at] = dot_nn(key, grad_scores)
        grad_value = dot_nt(grad[:, at], weights)
        grad_key = dot_nt(query[:, at], grad_scores)
        if start == 0:
            dk_acc[...] = grad_key
            dv_acc[...] = grad_value
        else:
            dk_acc[...] += grad_key
            dv_acc[...] += grad_value
    grad_query = dq_acc[...] * HD**-0.5
    grad_key = dk_acc[...] * HD**-0.5
    grad_value = dv_acc[...]
    if turned:
        grad_query = turn(grad_query, cos_ref[...], -sin_ref[...])
        grad_key = turn(grad_key, cos_ref[...], -sin_ref[...])
    keys = grad_key.shape[1]
    if valid < keys:
        real = lax.broadcasted_iota(jnp.int32, grad_key.shape, 1) < valid
        grad_key = jnp.where(real, grad_key, 0.0)
        grad_value = jnp.where(real, grad_value, 0.0)
    gain_ref[0, 0] = jnp.sum(grad_query * q_hat, axis=1, keepdims=True)
    gain_ref[0, 1] = jnp.sum(grad_key * k_hat, axis=1, keepdims=True)
    grad_query = lane_norm_back(grad_query, q_hat, q_inverse, qg_ref[...]).astype(BF16)
    grad_key = lane_norm_back(grad_key, k_hat, k_inverse, kg_ref[...]).astype(BF16)
    grads = [grad_key, grad_value.astype(BF16)]
    if turned:
        grads = [grad_query] + grads
    else:
        dq_ref[0] = grad_query
    for index, value in enumerate(grads):
        grads_ref[index, 0] = value


def head_block(array, first):
    return pl.BlockSpec((1,) + array.shape[1:], lambda h: (first + h, 0, 0))


def fixed(array):
    return pl.BlockSpec(array.shape, lambda h: (0,) * array.ndim)


def attend(q, k, v, starts, heads, qg, kg, angles, valid):
    tokens, keys = q.shape[2], k.shape[2]
    extra = list(angles)
    return pl.pallas_call(
        functools.partial(attend_kernel, bool(extra), valid),
        grid=(heads,),
        in_specs=[head_block(q, starts[0]), head_block(k, starts[1]), head_block(v, starts[2])]
        + [fixed(a) for a in [qg, kg] + extra],
        out_specs=[
            pl.BlockSpec((1, HD, tokens), lambda h: (h, 0, 0)),
            pl.BlockSpec((1, 1, tokens), lambda h: (h, 0, 0)),
        ],
        out_shape=[
            jax.ShapeDtypeStruct((heads, HD, tokens), BF16),
            jax.ShapeDtypeStruct((heads, 1, tokens), F32),
        ],
        compiler_params=pltpu.CompilerParams(vmem_limit_bytes=48 * 2**20),
        cost_estimate=cost("attend" if extra else "attend_cross"),
        name="attend",
    )(q, k, v, qg, kg, *extra)


def attend_back(q, k, v, starts, heads, qg, kg, angles, valid, out, lse, grad):
    tokens, keys = q.shape[2], k.shape[2]
    extra = list(angles)
    parts = 3 if extra else 2
    out_specs = [
        pl.BlockSpec((parts, 1, HD, keys), lambda h: (0, h, 0, 0)),
        pl.BlockSpec((1, 2, HD, 1), lambda h: (h, 0, 0, 0)),
    ]
    out_shape = [
        jax.ShapeDtypeStruct((parts, heads, HD, keys), BF16),
        jax.ShapeDtypeStruct((heads, 2, HD, 1), F32),
    ]
    if not extra:
        out_specs = [pl.BlockSpec((1, HD, tokens), lambda h: (h, 0, 0))] + out_specs
        out_shape = [jax.ShapeDtypeStruct((heads, HD, tokens), BF16)] + out_shape
    return pl.pallas_call(
        functools.partial(attend_back_kernel, bool(extra), valid),
        grid=(heads,),
        in_specs=[head_block(q, starts[0]), head_block(k, starts[1]), head_block(v, starts[2])]
        + [fixed(a) for a in [qg, kg] + extra]
        + [head_block(out, 0), head_block(lse, 0), head_block(grad, 0)],
        out_specs=out_specs,
        out_shape=out_shape,
        scratch_shapes=[
            pltpu.VMEM((HD, keys), F32),
            pltpu.VMEM((HD, keys), F32),
            pltpu.VMEM((HD, tokens), F32),
        ],
        compiler_params=pltpu.CompilerParams(vmem_limit_bytes=48 * 2**20),
        cost_estimate=cost("attend_back" if extra else "attend_back_cross"),
        name="attend_back",
    )(q, k, v, qg, kg, *extra, out, lse, grad)


CHUNK = 256


def core_pair(with_chip=False):
    group, chip, core = (lax.axis_index(axis) for axis in ("dp", "row", "col"))
    other, across = (group, chip, 1 - core), (group, 1 - chip, core)
    barrier = pltpu.get_barrier_semaphore()
    greeted = (other, across) if with_chip else (other,)
    for device in greeted:
        pl.semaphore_signal(barrier, inc=1, device_id=device, device_id_type=MESH)
    pl.semaphore_wait(barrier, len(greeted))
    return (other, across) if with_chip else other


def rows_at(step, base=0):
    return pl.ds(pl.multiple_of(base + step * CHUNK, CHUNK), CHUNK)


def send(src, dst, sems, step, other):
    return pltpu.make_async_remote_copy(
        src_ref=src,
        dst_ref=dst,
        send_sem=sems.at[0, step],
        recv_sem=sems.at[1, step],
        device_id=other,
        device_id_type=MESH,
    )


def join_rows(dst, own, far):
    size = own.shape[0]
    dst[:size] = own[...]
    dst[size:] = far[...]


def join_columns(dst, own, far):
    size = own.shape[1]
    dst[:, :size] = own[...]
    dst[:, size:] = far[...]


def row_norm(values):
    average = jnp.mean(values, axis=1, keepdims=True)
    variance = jnp.mean(values * values, axis=1, keepdims=True) - average * average
    inverse = lax.rsqrt(variance + EPSILON)
    return (values - average) * inverse, inverse


def row_norm_back(grad, normed, inverse, gain):
    scaled = grad * gain
    first = jnp.mean(scaled, axis=1, keepdims=True)
    second = jnp.mean(scaled * normed, axis=1, keepdims=True)
    return inverse * (scaled - first - normed * second)


GELU_A = 0.7978845608028654
GELU_B = 0.044715


def gelu_parts(pre):
    square = pre * pre
    angle = jnp.tanh(GELU_A * pre * (1.0 + GELU_B * square))
    value = 0.5 * pre * (1.0 + angle)
    slope = 0.5 * (1.0 + angle) + 0.5 * pre * (1.0 - angle * angle) * GELU_A * (
        1.0 + 3.0 * GELU_B * square
    )
    return value, slope


def steps(body, half):
    def one(step, carry):
        body(step)
        return carry

    lax.fori_loop(0, half // CHUNK, one, 0)


def skip_norm(half, lat, joint, gain, low, average_out, inverse_out, exchange, mine, theirs):
    tokens, width = lat.shape
    mine[...] = jnp.zeros_like(mine)

    def sums(step):
        at = rows_at(step)
        first, second = lat[at].astype(F32), joint[at].astype(F32)
        total = jnp.sum(first, axis=1, keepdims=True) + jnp.sum(second, axis=1, keepdims=True)
        square = jnp.sum(first * first, axis=1, keepdims=True) + jnp.sum(
            second * second, axis=1, keepdims=True
        )
        mine[at, 0:1] = total
        mine[at, 1:2] = square

    steps(sums, tokens)
    exchange.start()
    exchange.wait()
    begin = lax.axis_index("col") * half

    def norm(step):
        at = rows_at(step)
        place = pl.ds(pl.multiple_of(lax.rem(begin + step * CHUNK, tokens), CHUNK), CHUNK)
        average = (mine[place, 0:1] + theirs[place, 0:1]) * (1.0 / (2 * D))
        square = (mine[place, 1:2] + theirs[place, 1:2]) * (1.0 / (2 * D))
        inverse = lax.rsqrt(square - average * average + EPSILON)
        average_out[at] = average
        inverse_out[at] = inverse
        low[at, :width] = ((lat[place].astype(F32) - average) * inverse * gain[0:1]).astype(BF16)
        low[at, width:] = ((joint[place].astype(F32) - average) * inverse * gain[1:2]).astype(BF16)

    steps(norm, tokens)


def forward_kernel(tokens_last, residual, shifted, feed, fetch, *refs):
    refs = list(refs)
    take = lambda: refs.pop(0)
    if fetch:
        lat_ref, joint_ref, skip_gain = take(), take(), take()
    else:
        a_ref = take()
    w1o = take()
    w1f = None if fetch else take()
    gain = take()
    res_ref = take() if residual else None
    shift = take() if shifted else None
    w2o = take()
    w2f = None if fetch else take()
    if fetch:
        next_own = [take(), take()]
    if feed:
        w3o, w3f = take(), take()
    state_ref, x_ref, out_ref = take(), take(), take()
    if fetch:
        a_ref, average_ref, inverse_ref = take(), take(), take()
        next_far = [take(), take()]
    w1, w2, sent, got, sems, x_sems = take(), take(), take(), take(), take(), take()
    if feed:
        w3, sent_out, got_out, out_sems = take(), take(), take(), take()
    half = state_ref.shape[0]
    if fetch:
        w1f, w2f, far_sems, mine, theirs, stat_sems = (take() for _ in range(6))
        other, across = core_pair(True)
        owns, fars = [w1o, w2o] + next_own, [w1f, w2f] + next_far
        fetches = [
            send(own, far, far_sems, step, across) for step, (own, far) in enumerate(zip(owns, fars))
        ]
        for copy in fetches:
            copy.start()
        skip_norm(
            half, lat_ref, joint_ref, skip_gain, a_ref, average_ref, inverse_ref,
            send(mine, theirs, stat_sems, 0, other), mine, theirs,
        )
        fetches[0].wait_recv()
    else:
        other = core_pair()
    join_columns(w1, w1o, w1f)

    def rows_of(step, base):
        if tokens_last:
            return a_ref[:, rows_at(step, base)].T
        return a_ref[rows_at(step, base)]

    def give(step):
        at = rows_at(step)
        sent[at] = dot_nn(rows_of(step, half), w1[...])
        send(sent.at[at], got.at[at], sems, step, other).start()

    steps(give, half)
    if not fetch:
        join_rows(w2, w2o, w2f)
    if feed:
        join_rows(w3, w3o, w3f)

    def keep(step):
        at = rows_at(step)
        state = dot_nn(rows_of(step, 0), w1[...])
        if residual:
            state = state + res_ref[at]
        send(sent.at[at], got.at[at], sems, step, other).wait_recv()
        state = state + got[at]
        state_ref[at] = state
        x = row_norm(state)[0] * gain[...]
        if shifted:
            x = x + shift[...]
        x_ref[at] = x.astype(BF16)
        send(x_ref.at[at], x_ref.at[rows_at(step, half)], x_sems, step, other).start()

    steps(keep, half)
    if fetch:
        fetches[1].wait_recv()
        join_rows(w2, w2o, w2f)

    def arrive(step):
        at = rows_at(step)
        send(x_ref.at[at], x_ref.at[rows_at(step, half)], x_sems, step, other).wait_recv()

    if feed:

        def hidden(step, base):
            pre = dot_nn(x_ref[rows_at(step, base)], w2[...])
            return dot_nt(gelu_parts(pre)[0].astype(BF16), w3[...])

        def give_out(step):
            at = rows_at(step)
            arrive(step)
            sent_out[at] = hidden(step, half)
            send(sent_out.at[at], got_out.at[at], out_sems, step, other).start()

        steps(give_out, half)

        def keep_out(step):
            at = rows_at(step)
            value = hidden(step, 0) + state_ref[at]
            send(sent_out.at[at], got_out.at[at], out_sems, step, other).wait_recv()
            out_ref[at] = (value + got_out[at]).astype(BF16)

        steps(keep_out, half)
    else:

        def near_out(step):
            at = rows_at(step)
            out_ref[:, at] = dot_nn(x_ref[at], w2[...]).T

        steps(near_out, half)

        def far_out(step):
            arrive(step)
            at = rows_at(step, half)
            out_ref[:, at] = dot_nn(x_ref[at], w2[...]).T

        steps(far_out, half)

    def drain(step):
        at = rows_at(step)
        send(sent.at[at], got.at[at], sems, step, other).wait_send()
        send(x_ref.at[at], x_ref.at[rows_at(step, half)], x_sems, step, other).wait_send()
        if feed:
            send(sent_out.at[at], got_out.at[at], out_sems, step, other).wait_send()

    steps(drain, half)
    if fetch:
        for copy in fetches[2:]:
            copy.wait_recv()
        for copy in fetches:
            copy.wait_send()


def whole_call(kernel, operands, out_shape, scratch_shapes, collective, name):
    vmem = pl.BlockSpec(memory_space=pltpu.VMEM)
    return pl.pallas_call(
        kernel,
        in_specs=[vmem] * len(operands),
        out_specs=[vmem] * len(out_shape),
        out_shape=[jax.ShapeDtypeStruct(shape, dtype) for shape, dtype in out_shape],
        scratch_shapes=scratch_shapes,
        compiler_params=pltpu.CompilerParams(
            collective_id=collective, has_side_effects=True, vmem_limit_bytes=60 * 2**20
        ),
        cost_estimate=cost(name),
        name=name,
    )(*operands)


def pair_sems(half):
    return pltpu.SemaphoreType.DMA((2, half // CHUNK))


def forward_bridge(a, tokens_last, w1, gain, res, shift, w2, w3, collective, name, later=()):
    fetch = len(later) > 0
    tokens = a[0].shape[0] if fetch else a.shape[1]
    half = tokens // 2
    feed = w3 is not None
    operands = [*(a if fetch else (a,)), *w1, gain]
    operands += [res] if res is not None else []
    operands += [shift] if shift is not None else []
    operands += [*w2, *later] + ([*w3] if feed else [])
    depth, wide = w1[0].shape[0], w2[0].shape[1]
    out_shape = [((half, D), F32), ((tokens, D), BF16)]
    out_shape += [((half, D), BF16)] if feed else [((wide, tokens), F32)]
    part = pltpu.VMEM((half, D), F32)
    joined = [(depth, D), (D, wide)]
    scratch = [part, part, pair_sems(half), pair_sems(half)]
    if fetch:
        out_shape += [((tokens, depth), BF16), ((tokens, 1), F32), ((tokens, 1), F32)]
        out_shape += [(weight.shape, BF16) for weight in later]
        out_shape += [(shape, BF16) for shape in joined]
    else:
        scratch = [pltpu.VMEM(shape, BF16) for shape in joined] + scratch
    if feed:
        scratch += [pltpu.VMEM((D, wide), BF16), part, part, pair_sems(half)]
    if fetch:
        scratch += [
            pltpu.VMEM(w1[0].shape, BF16),
            pltpu.VMEM(w2[0].shape, BF16),
            pltpu.SemaphoreType.DMA((2, 2 + len(later))),
            pltpu.VMEM((tokens, 128), F32),
            pltpu.VMEM((tokens, 128), F32),
            pltpu.SemaphoreType.DMA((2, 1)),
        ]
    return whole_call(
        functools.partial(
            forward_kernel, tokens_last, res is not None, shift is not None, feed, fetch
        ),
        operands,
        out_shape,
        scratch,
        collective,
        name,
    )


def backward_kernel(feed, summed, tokens_last, whole, *refs):
    refs = list(refs)
    take = lambda: refs.pop(0)
    if feed:
        cot_ref, feed_ref, w3o, w3f = take(), take(), take(), take()
    else:
        g_ref, res_ref = take(), take()
    if whole:
        w2, state_ref, gain, w1 = take(), take(), take(), take()
    else:
        w2o, w2f, state_ref, gain, w1o, w1f = (take() for _ in range(6))
    if feed:
        hidden_ref, pre_ref = take(), take()
    total_ref, b_ref, out_ref, gain_ref = take(), take(), take(), take()
    if summed:
        sum_ref = take()
    if not whole:
        w1, w2 = take(), take()
    sent, got, sems, x_sems = take(), take(), take(), take()
    if feed:
        w3 = take()
    half = state_ref.shape[0]
    other = core_pair()
    if not whole:
        join_rows(w2, w2o, w2f)
    if feed:
        join_rows(w3, w3o, w3f)

    def part(step, base):
        at = rows_at(step, base)
        if feed:
            value, slope = gelu_parts(dot_nn(feed_ref[at], w2[...]))
            hidden_ref[at] = value.astype(BF16)
            rows = (dot_nn(cot_ref[at], w3[...]) * slope).astype(BF16)
            pre_ref[at] = rows
        else:
            rows = g_ref[:, at].T
        return dot_nt(rows, w2[...])

    def give(step):
        at = rows_at(step)
        sent[at] = part(step, half)
        send(sent.at[at], got.at[at], sems, step, other).start()

    steps(give, half)
    if not whole:
        join_columns(w1, w1o, w1f)
    gain_ref[...] = jnp.zeros_like(gain_ref)
    if summed:
        sum_ref[...] = jnp.zeros_like(sum_ref)

    def keep(step):
        at = rows_at(step)
        grad = part(step, 0)
        send(sent.at[at], got.at[at], sems, step, other).wait_recv()
        grad = grad + got[at]
        normed, inverse = row_norm(state_ref[at])
        gain_ref[...] += jnp.sum(grad * normed, axis=0, keepdims=True)
        if summed:
            sum_ref[...] += jnp.sum(grad, axis=0, keepdims=True)
        back = row_norm_back(grad, normed, inverse, gain[...])
        total = back + (cot_ref[at].astype(F32) if feed else res_ref[at])
        total_ref[at] = total
        b_ref[at] = total.astype(BF16)
        send(b_ref.at[at], b_ref.at[rows_at(step, half)], x_sems, step, other).start()

    steps(keep, half)

    def product(at):
        value = dot_nt(b_ref[at], w1[...])
        if tokens_last:
            out_ref[:, at] = value.T.astype(out_ref.dtype)
        else:
            out_ref[at] = value.astype(out_ref.dtype)

    def near_out(step):
        product(rows_at(step))

    steps(near_out, half)

    def far_out(step):
        at = rows_at(step)
        send(b_ref.at[at], b_ref.at[rows_at(step, half)], x_sems, step, other).wait_recv()
        product(rows_at(step, half))

    steps(far_out, half)

    def drain(step):
        at = rows_at(step)
        send(sent.at[at], got.at[at], sems, step, other).wait_send()
        send(b_ref.at[at], b_ref.at[rows_at(step, half)], x_sems, step, other).wait_send()

    steps(drain, half)


def backward_bridge(g, res, feed, w2, state, gain, w1, summed, tokens_last, collective, name):
    half = state.shape[0]
    tokens = 2 * half
    depth, wide = w2[0].shape[1], w1[0].shape[0]
    if feed:
        operands = [feed[0], feed[1], *feed[2]]
    else:
        operands = [g, res]
    operands += [*w2, state, gain, *w1]
    out_shape = [((tokens, depth), BF16)] * 2 if feed else []
    out_shape += [((half, D), F32), ((tokens, D), BF16)]
    out_shape += [((wide, tokens), BF16)] if tokens_last else [((tokens, wide), F32)]
    out_shape += [((1, D), F32)] * (2 if summed else 1)
    part = pltpu.VMEM((half, D), F32)
    scratch = [part, part, pair_sems(half), pair_sems(half)]
    whole = len(w1) == 1
    if not whole:
        scratch = [pltpu.VMEM((wide, D), BF16), pltpu.VMEM((D, depth), BF16)] + scratch
    if feed:
        scratch += [pltpu.VMEM((D, depth), BF16)]
    return whole_call(
        functools.partial(backward_kernel, bool(feed), summed, tokens_last, whole),
        operands,
        out_shape,
        scratch,
        collective,
        name,
    )


def product_kernel(by_rows, left_last, left_ref, right_ref, own_ref, far_ref):
    left, right = left_ref[...], right_ref[...]
    if by_rows:
        if left_last:
            value = dot_nn(left, right).T
        else:
            value = dot_tn(right, left)
        value = value.astype(BF16)
        size = value.shape[0] // 2
        parts = (value[:size], value[size:])
    else:
        value = dot_nn(left, right) if left_last else dot_tn(left, right)
        value = value.astype(BF16)
        size = value.shape[1] // 2
        parts = (value[:, :size], value[:, size:])
    for part, ref in zip(parts, (own_ref, far_ref)):
        rows, columns = ref.shape
        if part.shape == ref.shape:
            ref[...] = part
        else:
            ref[:, : columns // 2] = part[:rows]
            ref[:, columns // 2 :] = part[rows:]


def weight_product(left, left_last, right, by_rows, tile, name):
    wide = left.shape[0] if left_last else left.shape[1]
    tokens, across = right.shape
    if left_last:
        left_spec = pl.BlockSpec((tile, tokens), lambda i: (i, 0))
    else:
        left_spec = pl.BlockSpec((tokens, tile), lambda i: (0, i))
    rows = tile * across // 2 // D
    out_spec = pl.BlockSpec((rows, D), lambda i: (i, 0))
    out_shape = jax.ShapeDtypeStruct((rows * (wide // tile), D), BF16)
    return pl.pallas_call(
        functools.partial(product_kernel, by_rows, left_last),
        grid=(wide // tile,),
        in_specs=[left_spec, pl.BlockSpec((tokens, across), lambda i: (0, 0))],
        out_specs=[out_spec, out_spec],
        out_shape=[out_shape, out_shape],
        compiler_params=pltpu.CompilerParams(vmem_limit_bytes=48 * 2**20),
        cost_estimate=cost(name),
        name=name,
    )(left, right)


def pieces_of(rows):
    for pieces in (3, 2, 5):
        if rows % (16 * pieces) == 0:
            return pieces
    return 1


def ring_kernel(size, plan, *refs):
    refs = list(refs)
    sections = len(plan)

    def take(count):
        return [refs.pop(0) for _ in range(count)]

    own_refs = [take(len(parts)) for _, parts in plan]
    far_refs = [take(len(parts)) for _, parts in plan]
    out_refs = take(sections)
    work_refs = take(sections)
    slot_refs = take(sections)
    sends, arrivals, far_sems = take(3)
    index = lax.axis_index("dp")
    chip = lax.axis_index("row")
    core = lax.axis_index("col")
    across = size // 2
    side = lax.rem(index, 2)
    level = index // 2
    place = (1 - side) * level + side * (size - 1 - level)

    def device_at(where):
        where = lax.rem(where + size, size)
        turned = where // across
        high = (1 - turned) * where + turned * (size - 1 - where)
        return (high * 2 + turned, chip, core)

    neighbours = (device_at(place + 1), device_at(place - 1))
    partner = (index, 1 - chip, core)
    barrier = pltpu.get_barrier_semaphore()
    for device in neighbours + (partner,):
        pl.semaphore_signal(barrier, inc=1, device_id=device, device_id_type=MESH)
    pl.semaphore_wait(barrier, 3)

    exchanges = []
    for section in range(sections):
        exchanges.append([])
        if plan[section][0]:
            base = 0
            for number, far in enumerate(far_refs[section]):
                rows = far.shape[0]
                exchange = pltpu.make_async_remote_copy(
                    src_ref=far,
                    dst_ref=work_refs[section].at[base : base + rows],
                    send_sem=far_sems.at[0, section, number],
                    recv_sem=far_sems.at[1, section, number],
                    device_id=partner,
                    device_id_type=MESH,
                )
                exchange.start()
                exchanges[section].append(exchange)
                base += rows

    def ring(which, source, total, slots):
        half = source.shape[0] // 2
        rows = half // size
        pieces = pieces_of(rows)
        piece = rows // pieces

        def span(way, chunk, part):
            chunk = lax.rem(chunk + 2 * size, size)
            return pl.ds(pl.multiple_of(way * half + chunk * rows + part * piece, 16), piece)

        def chunk_of(way, step):
            return place - step if way == 0 else place + step

        def within(part):
            return pl.ds(part * piece, piece)

        def copy(way, part, step, src, dst, phase):
            return pltpu.make_async_remote_copy(
                src_ref=src,
                dst_ref=dst,
                send_sem=sends.at[which, phase, way, part, step],
                recv_sem=arrivals.at[which, phase, way, part, step],
                device_id=neighbours[way],
                device_id_type=MESH,
            )

        def first(way, part):
            src = source.at[span(way, chunk_of(way, 0), part)]
            return copy(way, part, 0, src, slots.at[way, 0, within(part)], 0)

        def reduced(way, part, step):
            src = slots.at[way, step - 1, within(part)]
            return copy(way, part, step, src, slots.at[way, step, within(part)], 0)

        def spread(way, part, step):
            at = span(way, chunk_of(way, step) + (1 if way == 0 else -1), part)
            return copy(way, part, step, total.at[at], total.at[at], 1)

        def arrival(way, part, step):
            return first(way, part) if isinstance(step, int) else reduced(way, part, step)

        def added(way, part, step):
            at = span(way, chunk_of(way, step + 1), part)
            got = slots[way, step, within(part)]
            return at, (source[at].astype(F32) + got.astype(F32)).astype(BF16)

        each = [(way, part) for part in range(pieces) for way in range(2)]
        for way, part in each:
            first(way, part).start()

        def reduce_step(step, carry):
            for way, part in each:
                arrival(way, part, step).wait_recv()
                _, value = added(way, part, step)
                slots[way, step, within(part)] = value
                reduced(way, part, step + 1).start()
            return carry

        reduce_step(0, 0)
        lax.fori_loop(1, size - 2, reduce_step, 0)
        for way, part in each:
            reduced(way, part, size - 2).wait_recv()
            at, value = added(way, part, size - 2)
            total[at] = value
            spread(way, part, 0).start()

        def gather_step(step, carry):
            for way, part in each:
                spread(way, part, step).wait_recv()
                spread(way, part, step + 1).start()
            return carry

        lax.fori_loop(0, size - 2, gather_step, 0)
        for way, part in each:
            spread(way, part, size - 2).wait_recv()
            first(way, part).wait_send()
            spread(way, part, 0).wait_send()

        def drain(step, carry):
            for way, part in each:
                reduced(way, part, step).wait_send()
                spread(way, part, step).wait_send()
            return carry

        lax.fori_loop(1, size - 1, drain, 0)

    for section in range(sections):
        exchanged, parts = plan[section]
        work = work_refs[section]
        base = 0
        for number, rows in enumerate(parts):
            own = own_refs[section][number][...]
            if exchanged:
                exchanges[section][number].wait()
                near = work[base : base + rows]
            else:
                near = far_refs[section][number][...]
            work[base : base + rows] = (own.astype(F32) + near.astype(F32)).astype(BF16)
            base += rows
        if base < work.shape[0]:
            work[base:] = jnp.zeros((work.shape[0] - base, work.shape[1]), BF16)
        ring(section, work, out_refs[section], slot_refs[section])


def ring_sum(size, sections):
    vmem = pl.BlockSpec(memory_space=pltpu.VMEM)
    plan = tuple((exchanged, tuple(own.shape[0] for own in owns)) for exchanged, owns, _ in sections)
    owns = [own for _, parts, _ in sections for own in parts]
    fars = [far for _, _, parts in sections for far in parts]
    totals = [sum(parts) for _, parts in plan]
    totals = [rows + -rows % (32 * size) for rows in totals]
    whole = [pltpu.VMEM((rows, D), BF16) for rows in totals]
    slots = [pltpu.VMEM((2, size - 1, rows // 2 // size, D), BF16) for rows in totals]
    pieces = max(pieces_of(rows // 2 // size) for rows in totals)
    sems = pltpu.SemaphoreType.DMA((len(sections), 2, 2, pieces, size - 1))
    most = max(len(parts) for _, parts in plan)
    return pl.pallas_call(
        functools.partial(ring_kernel, size, plan),
        in_specs=[vmem] * (len(owns) + len(fars)),
        out_specs=[vmem] * len(sections),
        out_shape=[jax.ShapeDtypeStruct((rows, D), BF16) for rows in totals],
        scratch_shapes=whole
        + slots
        + [sems, sems, pltpu.SemaphoreType.DMA((2, len(sections), most))],
        compiler_params=pltpu.CompilerParams(
            collective_id=0, has_side_effects=True, vmem_limit_bytes=62 * 2**20
        ),
        cost_estimate=cost("ring_sum"),
        name="ring_sum",
    )(*owns, *fars)


def shards(
    latents,
    skip_input,
    condition,
    text_states,
    positions,
    cotangent,
    skip_gain,
    skip_weight,
    shift_weight,
    self_gain,
    self_weight,
    query_gain,
    key_gain,
    self_out,
    cross_gain,
    cross_query,
    cross_context,
    cross_query_gain,
    cross_key_gain,
    cross_out,
    feed_gain,
    up_weight,
    down_weight,
):
    tokens, width = latents.shape
    half = tokens // 2
    heads_here = width // HD
    core = lax.axis_index("col")
    chip = lax.axis_index("row")
    straight = core == chip

    def own_first(values):
        return (
            lax.dynamic_slice_in_dim(values, core * half, half, 0),
            lax.dynamic_slice_in_dim(values, (1 - core) * half, half, 0),
        )

    def in_order(own, other):
        return jnp.where(
            core == 0, jnp.concatenate([own, other]), jnp.concatenate([other, own])
        )

    skip_flat = skip_weight.reshape(2 * width, -1)
    self_flat = self_weight.reshape(-1, 3 * width)
    context_flat = cross_context.reshape(-1, 2 * width)

    rows = up_weight.shape[0]
    norm_far = other_chip(jnp.stack([self_gain, cross_gain, feed_gain]))

    def near_and_far(weight):
        return (weight, other_chip(weight))

    def share_of(weight):
        share = weight.shape[0] // lax.axis_size("dp")
        piece = lax.dynamic_slice_in_dim(weight, lax.axis_index("dp") * share, share, 0)
        return other_chip(piece)

    down_turned = down_weight.T
    up_share, down_share = share_of(up_weight), share_of(down_turned)
    up_pair = (up_weight, lax.all_gather(up_share, "dp", axis=0, tiled=True))
    down_pair = (down_turned, lax.all_gather(down_share, "dp", axis=0, tiled=True))
    norm_gains = jnp.concatenate([jnp.stack([self_gain, cross_gain, feed_gain]), norm_far], axis=1)
    self_gain_all, cross_gain_all, feed_gain_all = norm_gains[0:1], norm_gains[1:2], norm_gains[2:3]

    text_near = other_core(text_states)
    text_mine = jnp.where(straight, text_states, text_near)
    text_here = text_states.shape[0]
    kept, handed = own_first(cotangent)
    handed = other_core(handed)
    cot_mine = jnp.where(straight, kept, handed)

    place_own, place_other = own_first(positions)
    places = jnp.concatenate([place_own, place_other]).astype(F32)
    quarter = HD // 4
    frequency = 10000.0 ** (-jnp.arange(quarter, dtype=F32) / quarter)
    angles = frequency[:, None] * places.T[:, None, :]
    cosine = jnp.cos(angles)
    sine = jnp.sin(angles)
    cosine = jnp.stack([cosine, cosine], axis=1).reshape(HD, tokens)
    sine = jnp.stack([-sine, sine], axis=1).reshape(HD, tokens)

    lat_own, lat_other = own_first(latents)
    skip_own, skip_other = own_first(skip_input)
    lat = jnp.concatenate([lat_own, lat_other]).astype(F32)
    joint = jnp.concatenate([skip_own, skip_other]).astype(F32)

    def swap_halves(values):
        return jnp.concatenate([values[:, half:], values[:, :half]], axis=1)

    cond_low = jax.nn.silu(condition.astype(F32)).astype(BF16)
    shift_part = contract(cond_low, shift_weight)
    shift_part = shift_part + other_core(shift_part)
    shift_mine = lax.dynamic_slice_in_dim(shift_part, chip, 1, 0)
    shift_far = other_chip(lax.dynamic_slice_in_dim(shift_part, 1 - chip, 1, 0))
    shift_row = jnp.concatenate([shift_mine, shift_far], axis=1)

    (
        first_state,
        first_all,
        mixed_raw,
        skip_low,
        average,
        skip_inverse,
        out_far_half,
        query_far_half,
        skip_whole,
        self_whole,
    ) = forward_bridge(
        (latents, skip_input, skip_gain), False, (skip_flat,), self_gain_all, None, shift_row, (self_flat,), None, 1, "into_self",
        (self_out, cross_query),
    )
    mixed_raw = mixed_raw.reshape(3 * heads_here, HD, tokens)


    def fetched(values, gate):
        return other_chip(after(values, gate))

    out_pair = (self_out, out_far_half)
    query_pair = (cross_query, query_far_half)
    text_far = fetched(jnp.where(straight, text_near, text_states), first_all)
    context_far = fetched(context_flat, text_far)
    cross_pair = (cross_out, fetched(cross_out, text_far))
    mixed_raw = after(mixed_raw, text_far)
    self_args = (
        (mixed_raw, mixed_raw, mixed_raw),
        (0, heads_here, 2 * heads_here),
        heads_here,
        query_gain[:, None],
        key_gain[:, None],
        (cosine, sine),
        tokens,
    )
    heads_low, log_first = attend(*self_args[0], *self_args[1:])
    heads_flat = heads_low.reshape(width, tokens)
    cot_far = fetched(jnp.where(straight, handed, kept), heads_low)
    second_state, cross_all, probe_raw = forward_bridge(
        heads_flat, True, out_pair, cross_gain_all, first_state, None, query_pair, None, 2, "into_cross"
    )
    probe_raw = probe_raw.reshape(heads_here, HD, tokens)
    text_far, context_far = after((text_far, context_far), cross_all)
    text_all = jnp.concatenate([text_mine, text_far], axis=1)
    text_all = jnp.pad(text_all, ((0, -text_here % 128), (0, 0)))
    context_all = jnp.concatenate([context_flat, context_far])
    memory_raw = lax.dot_general(
        context_all, text_all, (((0,), (1,)), ((), ())), preferred_element_type=F32
    ).reshape(2 * heads_here, HD, -1)
    cross_args = (
        (probe_raw, memory_raw, memory_raw),
        (0, 0, heads_here),
        heads_here,
        cross_query_gain[:, None],
        cross_key_gain[:, None],
        (),
        text_here,
    )
    cross_low, log_second = attend(*cross_args[0], *cross_args[1:])
    cross_flat = cross_low.reshape(width, tokens)
    third_state, feed_all, out_own = forward_bridge(
        cross_flat, True, cross_pair, feed_gain_all, second_state, None, up_pair, down_pair, 3, "into_feed"
    )
    row_width = up_weight.shape[0]
    out_mine = out_own[:, :row_width]
    out_far = other_chip(out_own[:, row_width:])

    cot_own = jnp.concatenate([cot_mine, after(cot_far, feed_all)], axis=1)
    cot_all = pair(cot_own)
    (
        hidden_low,
        grad_pre,
        grad_third,
        branch_two_all,
        grad_cross_heads,
        feed_gain_part,
    ) = backward_bridge(
        None,
        None,
        (cot_all, feed_all, down_pair),
        up_pair,
        third_state,
        feed_gain_all,
        cross_pair,
        False,
        True,
        4,
        "from_feed",
    )
    down_own, down_far = weight_product(hidden_low, False, cot_all, True, 1152, "grad_down")
    up_own, up_far = weight_product(grad_pre, False, feed_all, True, 1152, "grad_up")
    cross_own, cross_far = weight_product(
        cross_flat, True, branch_two_all, False, 576, "grad_cross_out"
    )
    down_far_here = other_chip(down_far)
    up_far_here = other_chip(up_far)
    grad_cross_heads = after(grad_cross_heads, (down_far, up_far))
    grad_probe, grad_memory, grad_cross_gains = attend_back(
        *cross_args[0],
        *cross_args[1:],
        cross_low,
        log_second,
        grad_cross_heads.reshape(heads_here, HD, tokens),
    )
    probe_low = grad_probe.reshape(width, tokens)
    query_own, query_far = weight_product(probe_low, True, cross_all, True, 576, "grad_cross_query")
    memory_low = grad_memory.reshape(2 * width, -1)
    context_own, context_far = weight_product(
        memory_low, True, text_all, True, 576, "grad_context"
    )
    early_own = jnp.concatenate([cross_own, query_own, context_own])
    early_far = jnp.concatenate([cross_far, query_far, context_far])
    early_here = other_chip(early_far)
    probe_low = after(probe_low, early_far)
    text_part = lax.dot_general(
        memory_low, context_all, (((0,), (1,)), ((), ())), preferred_element_type=F32
    )[:text_here]
    text_width = text_states.shape[1]
    text_one, text_two = text_part[:, :text_width], text_part[:, text_width:]
    text_sum = jnp.where(straight, text_one, text_two) + other_core(
        jnp.where(straight, text_two, text_one)
    )
    text_sum = text_sum.astype(BF16)
    text_back = lax.ppermute(text_sum, ("row", "col"), [(1, 2), (2, 1)])

    grad_second, branch_one_all, grad_heads, cross_gain_part = backward_bridge(
        probe_low,
        grad_third,
        None,
        query_pair,
        second_state,
        cross_gain_all,
        out_pair,
        False,
        True,
        5,
        "from_cross",
    )
    out_grad_own, out_grad_far = weight_product(
        heads_flat, True, branch_one_all, False, 576, "grad_self_out"
    )

    def summed(own, far):
        return (own.astype(F32) + far.astype(F32)).astype(BF16)

    down_sum = summed(down_own, after(down_far_here, grad_heads))
    down_share = lax.psum_scatter(down_sum, "dp", scatter_dimension=0, tiled=True)
    grad_heads_in = after(grad_heads, down_sum)
    grad_mixed, grad_self_gains = attend_back(
        *self_args[0],
        *self_args[1:],
        heads_low,
        log_first,
        grad_heads_in.reshape(heads_here, HD, tokens),
    )
    mixed_low = grad_mixed.reshape(3 * width, tokens)
    up_sum = summed(up_own, up_far_here)
    mixed_in = after(mixed_low, (down_share, up_sum))
    self_own, self_far = weight_product(mixed_low, True, first_all, True, 576, "grad_self")
    _, grad_first_all, grad_skip_out, self_gain_part, shift_grad = backward_bridge(
        mixed_in,
        grad_second,
        None,
        (self_whole,),
        first_state,
        self_gain_all,
        (skip_whole,),
        True,
        False,
        6,
        "from_self",
    )
    skip_own, skip_far = weight_product(skip_low, False, grad_first_all, False, 384, "grad_skip")
    shift_grad = shift_grad + other_core(shift_grad)
    shift_here = shift_grad[:, :row_width]
    shift_there = other_chip(shift_grad[:, row_width:])
    shift_pair = jnp.where(
        chip == 0,
        jnp.concatenate([shift_here, shift_there]),
        jnp.concatenate([shift_there, shift_here]),
    )
    out_far = after(out_far, grad_skip_out)
    out_kept = jnp.where(straight, out_mine, out_far)
    out_got = other_core(jnp.where(straight, out_far, out_mine))
    block_out = in_order(out_kept, out_got)
    lat_normed = (lat - average) * skip_inverse
    joint_normed = (joint - average) * skip_inverse
    grad_lat, grad_joint = grad_skip_out[:, :width], grad_skip_out[:, width:]
    lat_scaled, joint_scaled = grad_lat * skip_gain[0], grad_joint * skip_gain[1]
    sums_back = jnp.stack(
        [
            jnp.sum(lat_scaled, axis=1) + jnp.sum(joint_scaled, axis=1),
            jnp.sum(lat_scaled * lat_normed, axis=1) + jnp.sum(joint_scaled * joint_normed, axis=1),
        ]
    )
    sums_back = sums_back + swap_halves(other_core(sums_back))
    first_mean = (sums_back[0] / (2 * D))[:, None]
    second_mean = (sums_back[1] / (2 * D))[:, None]
    skip_gain_part = jnp.stack(
        [jnp.sum(grad_lat * lat_normed, axis=0), jnp.sum(grad_joint * joint_normed, axis=0)]
    )
    grad_lat = (skip_inverse * (lat_scaled - first_mean - lat_normed * second_mean)).astype(BF16)
    grad_joint = (skip_inverse * (joint_scaled - first_mean - joint_normed * second_mean)).astype(BF16)
    grad_latents = in_order(grad_lat[:half], grad_lat[half:])
    grad_skip_input = in_order(grad_joint[:half], grad_joint[half:])

    wide = jnp.concatenate([self_gain_part, cross_gain_part, feed_gain_part])
    wide = wide + other_core(wide)
    narrow = jnp.concatenate([jnp.sum(grad_self_gains, axis=0), jnp.sum(grad_cross_gains, axis=0)])
    narrow = narrow[:, :, 0]
    narrow = narrow + other_core(narrow)

    def flat(*pieces):
        return jnp.concatenate([piece.reshape(-1) for piece in pieces])

    kept_gains = flat(wide[:, :row_width], narrow, skip_gain_part)
    sent_gains = flat(wide[:, row_width:], narrow, skip_gain_part)
    small = flat(
        kept_gains + other_chip(sent_gains), cond_low.astype(F32), shift_pair
    )
    groups = lax.axis_size("dp")
    smalls = [small] + [
        lax.ppermute(small, "dp", [(i, (i + k) % groups) for i in range(groups)])
        for k in range(1, groups)
    ]
    skip_own = after(skip_own, (grad_latents, grad_skip_input, block_out, small))
    middle, inner, last = ring_sum(
        groups,
        [
            (False, [early_own], [early_here]),
            (True, [out_grad_own, self_own], [out_grad_far, self_far]),
            (True, [skip_own], [skip_far]),
        ],
    )
    high = lax.psum(up_sum, "dp")
    low = lax.all_gather(down_share, "dp", axis=0, tiled=True)

    def unpack(block, count):
        rows = block.shape[0] // count
        pieces = [block[i * rows : (i + 1) * rows] for i in range(count)]
        return [
            jnp.concatenate([piece[:, :width], piece[:, width:]]).astype(F32) for piece in pieces
        ]


    def side_by_side(blocks):
        return jnp.concatenate([blocks[:row_width], blocks[row_width:]], axis=1).astype(F32)

    grad_down = side_by_side(low).T
    grad_up = side_by_side(high)
    place = width // 2
    grad_cross_out, grad_cross_query = unpack(middle[: 2 * place], 2)
    grad_context = jnp.concatenate(unpack(middle[2 * place : 2 * place + text_width], 2), axis=1)
    (grad_self_out,) = unpack(inner[:place], 1)
    grad_self_weight = jnp.stack(unpack(inner[place : 4 * place], 3), axis=1)
    grad_skip_weight = jnp.concatenate(unpack(last[: 2 * place], 3))

    grad_text_states = jnp.where(straight, text_sum, after(text_back, last))

    smalls = [after(value, last) for value in smalls[1:]] + smalls[:1]
    gain_count = kept_gains.shape[0]
    gain_sums = sum(value[:gain_count] for value in smalls)
    images = condition.shape[0]
    conds = [
        value[gain_count : gain_count + images * width].reshape(images, width) for value in smalls
    ]
    shifts = [value[gain_count + images * width :].reshape(images, row_width) for value in smalls]
    grad_shift_weight = lax.dot_general(
        jnp.concatenate(conds),
        jnp.concatenate(shifts),
        (((0,), (0,)), ((), ())),
        precision=PRECISE,
        preferred_element_type=F32,
    )
    wide_sum = gain_sums[: 3 * row_width].reshape(3, row_width)
    narrow_sum = gain_sums[3 * row_width : 3 * row_width + 4 * HD].reshape(4, HD)
    grad_skip_gain = gain_sums[3 * row_width + 4 * HD :].reshape(2, width)

    return (
        block_out,
        grad_latents,
        grad_skip_input,
        grad_text_states,
        grad_skip_gain,
        grad_skip_weight.reshape(skip_weight.shape),
        grad_shift_weight,
        wide_sum[0],
        grad_self_weight.reshape(self_weight.shape),
        narrow_sum[0],
        narrow_sum[1],
        grad_self_out,
        wide_sum[1],
        grad_cross_query,
        grad_context.reshape(cross_context.shape),
        narrow_sum[2],
        narrow_sum[3],
        grad_cross_out,
        wide_sum[2],
        grad_up,
        grad_down,
    )


def solution(mesh):
    placed = (
        P(("dp", "row"), "col"),
        P(("dp", "row"), "col"),
        P("dp", "col"),
        P(("dp", "col"), "row"),
        P(("dp", "row"), None),
        P(("dp", "col"), "row"),
        P(None, "col"),
        P(None, "col", "row"),
        P("col", "row"),
        P("row"),
        P("row", None, "col"),
        P(),
        P(),
        P("col", "row"),
        P("row"),
        P("row", "col"),
        P("row", None, "col"),
        P(),
        P(),
        P("col", "row"),
        P("row"),
        P("row", "col"),
        P("col", "row"),
    )
    return jax.shard_map(
        shards,
        mesh=mesh,
        in_specs=placed,
        out_specs=(
            P(("dp", "col"), "row"),
            P(("dp", "row"), "col"),
            P(("dp", "row"), "col"),
            P(("dp", "col"), "row"),
            P(None, "col"),
            P(None, "col", "row"),
            P("col", "row"),
            P("row"),
            P("row", None, "col"),
            P(),
            P(),
            P("col", "row"),
            P("row"),
            P("row", "col"),
            P("row", None, "col"),
            P(),
            P(),
            P("col", "row"),
            P("row"),
            P("row", "col"),
            P("col", "row"),
        ),
        check_vma=False,
    )
```

```python
import functools

import jax
import jax.numpy as jnp
from jax import lax
from jax.experimental import pallas as pl
from jax.experimental.pallas import tpu as pltpu
from jax.sharding import PartitionSpec as P

D = 1152
HD = 72
TXT = 333
LAT = 1024


EPSILON = 1e-06
PRECISE = lax.Precision.HIGHEST
SWAP = [(0, 1), (1, 0)]
BF16 = jnp.bfloat16
F32 = jnp.float32
MESH = pl.DeviceIdType.MESH
LOG2E = 1.4426950408889634
TIMES = {
    "attend": 15,
    "attend_cross": 7,
    "attend_back": 29,
    "attend_back_cross": 16,
    "into_self": 90,
    "into_cross": 15,
    "into_feed": 28,
    "from_feed": 40,
    "from_cross": 16,
    "from_self": 22,
    "grad_down": 9,
    "grad_up": 9,
    "grad_cross_out": 3,
    "grad_cross_query": 3,
    "grad_context": 3,
    "grad_self_out": 3,
    "grad_self": 8,
    "grad_skip": 6,
    "ring_sum": 200,
}
SHARE = 3.0


def cost(name):
    return pl.CostEstimate(
        flops=0, bytes_accessed=int(TIMES[name] * 3.69e6 / SHARE), transcendentals=0
    )


def other_core(values):
    return lax.ppermute(values, "col", SWAP)


def other_chip(values):
    return lax.ppermute(values, "row", SWAP)


def contract(left_side, right_side):
    return jnp.dot(left_side, right_side, preferred_element_type=F32)


def pair(own):
    return jnp.concatenate([own, other_core(own)])


def after(values, earlier):
    return lax.optimization_barrier((values, earlier))[0]


def dot_nn(a, b):
    return lax.dot_general(a, b, (((1,), (0,)), ((), ())), preferred_element_type=F32)


def dot_tn(a, b):
    return lax.dot_general(a, b, (((0,), (0,)), ((), ())), preferred_element_type=F32)


def dot_nt(a, b):
    return lax.dot_general(a, b, (((1,), (1,)), ((), ())), preferred_element_type=F32)


def lane_norm(values):
    average = jnp.mean(values, axis=0, keepdims=True)
    variance = jnp.mean(values * values, axis=0, keepdims=True) - average * average
    inverse = lax.rsqrt(variance + EPSILON)
    return (values - average) * inverse, inverse


def lane_norm_back(grad, normed, inverse, gain):
    scaled = grad * gain
    first = jnp.mean(scaled, axis=0, keepdims=True)
    second = jnp.mean(scaled * normed, axis=0, keepdims=True)
    return inverse * (scaled - first - normed * second)


def turn(values, cosine, sine):
    quarter = HD // 4
    place = lax.broadcasted_iota(jnp.int32, values.shape, 0)
    leading = (place < quarter) | ((place >= 2 * quarter) & (place < 3 * quarter))
    partner = jnp.where(
        leading,
        pltpu.roll(values, HD - quarter, 0),
        pltpu.roll(values, quarter, 0),
    )
    return values * cosine + partner * sine


def attend_kernel(turned, valid, q_ref, k_ref, v_ref, qg_ref, kg_ref, *rest):
    if turned:
        cos_ref, sin_ref, out_ref, lse_ref = rest
    else:
        out_ref, lse_ref = rest
    query = lane_norm(q_ref[0])[0] * qg_ref[...]
    key = lane_norm(k_ref[0])[0] * kg_ref[...]
    if turned:
        query = turn(query, cos_ref[...], sin_ref[...])
        key = turn(key, cos_ref[...], sin_ref[...])
    query = query.astype(BF16)
    key_rows = key.astype(BF16).T
    value = v_ref[0].astype(BF16)
    keys = value.shape[1]
    ones = jnp.ones((8, keys), BF16)
    if valid < keys:
        ones = jnp.where(lax.broadcasted_iota(jnp.int32, (8, keys), 1) < valid, 1.0, 0.0).astype(BF16)
    tokens = query.shape[1]
    block = 256
    for start in range(0, tokens, block):
        scores = dot_nn(key_rows, query[:, start : start + block])
        weights = jnp.exp2(scores * (LOG2E * HD**-0.5)).astype(BF16)
        total = dot_nn(ones, weights)[:1]
        out = dot_nn(value, weights)
        out_ref[0, :, start : start + block] = (out * (1.0 / total)).astype(BF16)
        lse_ref[0, :, start : start + block] = jnp.log2(total)


def attend_back_kernel(turned, valid, q_ref, k_ref, v_ref, qg_ref, kg_ref, *rest):
    if turned:
        cos_ref, sin_ref, out_ref, lse_ref, grad_ref, grads_ref, gain_ref, dk_acc, dv_acc, dq_acc = rest
    else:
        out_ref, lse_ref, grad_ref, dq_ref, grads_ref, gain_ref, dk_acc, dv_acc, dq_acc = rest
    q_hat, q_inverse = lane_norm(q_ref[0])
    k_hat, k_inverse = lane_norm(k_ref[0])
    query = q_hat * qg_ref[...]
    key = k_hat * kg_ref[...]
    if turned:
        query = turn(query, cos_ref[...], sin_ref[...])
        key = turn(key, cos_ref[...], sin_ref[...])
    query = query.astype(BF16)
    key = key.astype(BF16)
    key_rows = key.T
    value_rows = v_ref[0].astype(BF16).T
    grad = grad_ref[0]
    inner = jnp.sum(grad.astype(F32) * out_ref[0].astype(F32), axis=0, keepdims=True)
    tokens = query.shape[1]
    block = 256
    for start in range(0, tokens, block):
        at = slice(start, start + block)
        scores = dot_nn(key_rows, query[:, at])
        weights = jnp.exp2(scores * (LOG2E * HD**-0.5) - lse_ref[0, :, at])
        grad_weights = dot_nn(value_rows, grad[:, at])
        grad_scores = (weights * (grad_weights - inner[:, at])).astype(BF16)
        weights = weights.astype(BF16)
        dq_acc[:, at] = dot_nn(key, grad_scores)
        grad_value = dot_nt(grad[:, at], weights)
        grad_key = dot_nt(query[:, at], grad_scores)
        if start == 0:
            dk_acc[...] = grad_key
            dv_acc[...] = grad_value
        else:
            dk_acc[...] += grad_key
            dv_acc[...] += grad_value
    grad_query = dq_acc[...] * HD**-0.5
    grad_key = dk_acc[...] * HD**-0.5
    grad_value = dv_acc[...]
    if turned:
        grad_query = turn(grad_query, cos_ref[...], -sin_ref[...])
        grad_key = turn(grad_key, cos_ref[...], -sin_ref[...])
    keys = grad_key.shape[1]
    if valid < keys:
        real = lax.broadcasted_iota(jnp.int32, grad_key.shape, 1) < valid
        grad_key = jnp.where(real, grad_key, 0.0)
        grad_value = jnp.where(real, grad_value, 0.0)
    gain_ref[0, 0] = jnp.sum(grad_query * q_hat, axis=1, keepdims=True)
    gain_ref[0, 1] = jnp.sum(grad_key * k_hat, axis=1, keepdims=True)
    grad_query = lane_norm_back(grad_query, q_hat, q_inverse, qg_ref[...]).astype(BF16)
    grad_key = lane_norm_back(grad_key, k_hat, k_inverse, kg_ref[...]).astype(BF16)
    grads = [grad_key, grad_value.astype(BF16)]
    if turned:
        grads = [grad_query] + grads
    else:
        dq_ref[0] = grad_query
    for index, value in enumerate(grads):
        grads_ref[index, 0] = value


def head_block(array, first):
    return pl.BlockSpec((1,) + array.shape[1:], lambda h: (first + h, 0, 0))


def fixed(array):
    return pl.BlockSpec(array.shape, lambda h: (0,) * array.ndim)


def attend(q, k, v, starts, heads, qg, kg, angles, valid):
    tokens, keys = q.shape[2], k.shape[2]
    extra = list(angles)
    return pl.pallas_call(
        functools.partial(attend_kernel, bool(extra), valid),
        grid=(heads,),
        in_specs=[head_block(q, starts[0]), head_block(k, starts[1]), head_block(v, starts[2])]
        + [fixed(a) for a in [qg, kg] + extra],
        out_specs=[
            pl.BlockSpec((1, HD, tokens), lambda h: (h, 0, 0)),
            pl.BlockSpec((1, 1, tokens), lambda h: (h, 0, 0)),
        ],
        out_shape=[
            jax.ShapeDtypeStruct((heads, HD, tokens), BF16),
            jax.ShapeDtypeStruct((heads, 1, tokens), F32),
        ],
        compiler_params=pltpu.CompilerParams(vmem_limit_bytes=48 * 2**20),
        cost_estimate=cost("attend" if extra else "attend_cross"),
        name="attend",
    )(q, k, v, qg, kg, *extra)


def attend_back(q, k, v, starts, heads, qg, kg, angles, valid, out, lse, grad):
    tokens, keys = q.shape[2], k.shape[2]
    extra = list(angles)
    parts = 3 if extra else 2
    out_specs = [
        pl.BlockSpec((parts, 1, HD, keys), lambda h: (0, h, 0, 0)),
        pl.BlockSpec((1, 2, HD, 1), lambda h: (h, 0, 0, 0)),
    ]
    out_shape = [
        jax.ShapeDtypeStruct((parts, heads, HD, keys), BF16),
        jax.ShapeDtypeStruct((heads, 2, HD, 1), F32),
    ]
    if not extra:
        out_specs = [pl.BlockSpec((1, HD, tokens), lambda h: (h, 0, 0))] + out_specs
        out_shape = [jax.ShapeDtypeStruct((heads, HD, tokens), BF16)] + out_shape
    return pl.pallas_call(
        functools.partial(attend_back_kernel, bool(extra), valid),
        grid=(heads,),
        in_specs=[head_block(q, starts[0]), head_block(k, starts[1]), head_block(v, starts[2])]
        + [fixed(a) for a in [qg, kg] + extra]
        + [head_block(out, 0), head_block(lse, 0), head_block(grad, 0)],
        out_specs=out_specs,
        out_shape=out_shape,
        scratch_shapes=[
            pltpu.VMEM((HD, keys), F32),
            pltpu.VMEM((HD, keys), F32),
            pltpu.VMEM((HD, tokens), F32),
        ],
        compiler_params=pltpu.CompilerParams(vmem_limit_bytes=48 * 2**20),
        cost_estimate=cost("attend_back" if extra else "attend_back_cross"),
        name="attend_back",
    )(q, k, v, qg, kg, *extra, out, lse, grad)


CHUNK = 512


def core_pair(with_chip=False):
    group, chip, core = (lax.axis_index(axis) for axis in ("dp", "row", "col"))
    other, across = (group, chip, 1 - core), (group, 1 - chip, core)
    barrier = pltpu.get_barrier_semaphore()
    greeted = (other, across) if with_chip else (other,)
    for device in greeted:
        pl.semaphore_signal(barrier, inc=1, device_id=device, device_id_type=MESH)
    pl.semaphore_wait(barrier, len(greeted))
    return (other, across) if with_chip else other


def rows_at(step, base=0):
    return pl.ds(pl.multiple_of(base + step * CHUNK, CHUNK), CHUNK)


def send(src, dst, sems, step, other):
    return pltpu.make_async_remote_copy(
        src_ref=src,
        dst_ref=dst,
        send_sem=sems.at[0, step],
        recv_sem=sems.at[1, step],
        device_id=other,
        device_id_type=MESH,
    )


def join_rows(dst, own, far):
    size = own.shape[0]
    dst[:size] = own[...]
    dst[size:] = far[...]


def join_columns(dst, own, far):
    size = own.shape[1]
    dst[:, :size] = own[...]
    dst[:, size:] = far[...]


def row_norm(values):
    average = jnp.mean(values, axis=1, keepdims=True)
    variance = jnp.mean(values * values, axis=1, keepdims=True) - average * average
    inverse = lax.rsqrt(variance + EPSILON)
    return (values - average) * inverse, inverse


def row_norm_back(grad, normed, inverse, gain):
    scaled = grad * gain
    first = jnp.mean(scaled, axis=1, keepdims=True)
    second = jnp.mean(scaled * normed, axis=1, keepdims=True)
    return inverse * (scaled - first - normed * second)


GELU_A = 0.7978845608028654
GELU_B = 0.044715


def gelu_parts(pre):
    square = pre * pre
    angle = jnp.tanh(GELU_A * pre * (1.0 + GELU_B * square))
    value = 0.5 * pre * (1.0 + angle)
    slope = 0.5 * (1.0 + angle) + 0.5 * pre * (1.0 - angle * angle) * GELU_A * (
        1.0 + 3.0 * GELU_B * square
    )
    return value, slope


def steps(body, half):
    def one(step, carry):
        body(step)
        return carry

    lax.fori_loop(0, half // CHUNK, one, 0)


def skip_norm(half, lat, joint, gain, low, average_out, inverse_out, exchange, mine, theirs):
    tokens, width = lat.shape
    mine[...] = jnp.zeros_like(mine)

    def sums(step):
        at = rows_at(step)
        first, second = lat[at].astype(F32), joint[at].astype(F32)
        total = jnp.sum(first, axis=1, keepdims=True) + jnp.sum(second, axis=1, keepdims=True)
        square = jnp.sum(first * first, axis=1, keepdims=True) + jnp.sum(
            second * second, axis=1, keepdims=True
        )
        mine[at, 0:1] = total
        mine[at, 1:2] = square

    steps(sums, tokens)
    exchange.start()
    exchange.wait()
    begin = lax.axis_index("col") * half

    def norm(step):
        at = rows_at(step)
        place = pl.ds(pl.multiple_of(lax.rem(begin + step * CHUNK, tokens), CHUNK), CHUNK)
        average = (mine[place, 0:1] + theirs[place, 0:1]) * (1.0 / (2 * D))
        square = (mine[place, 1:2] + theirs[place, 1:2]) * (1.0 / (2 * D))
        inverse = lax.rsqrt(square - average * average + EPSILON)
        average_out[at] = average
        inverse_out[at] = inverse
        low[at, :width] = ((lat[place].astype(F32) - average) * inverse * gain[0:1]).astype(BF16)
        low[at, width:] = ((joint[place].astype(F32) - average) * inverse * gain[1:2]).astype(BF16)

    steps(norm, tokens)


def forward_kernel(tokens_last, residual, shifted, feed, fetch, *refs):
    refs = list(refs)
    take = lambda: refs.pop(0)
    if fetch:
        lat_ref, joint_ref, skip_gain = take(), take(), take()
    else:
        a_ref = take()
    w1o = take()
    w1f = None if fetch else take()
    gain = take()
    res_ref = take() if residual else None
    shift = take() if shifted else None
    w2o = take()
    w2f = None if fetch else take()
    if fetch:
        next_own = [take(), take()]
    if feed:
        w3o, w3f = take(), take()
    state_ref, x_ref, out_ref = take(), take(), take()
    if fetch:
        a_ref, average_ref, inverse_ref = take(), take(), take()
        next_far = [take(), take()]
    w1, w2, sent, got, sems, x_sems = take(), take(), take(), take(), take(), take()
    if feed:
        w3, sent_out, got_out, out_sems = take(), take(), take(), take()
    half = state_ref.shape[0]
    if fetch:
        w1f, w2f, far_sems, mine, theirs, stat_sems = (take() for _ in range(6))
        other, across = core_pair(True)
        owns, fars = [w1o, w2o] + next_own, [w1f, w2f] + next_far
        fetches = [
            send(own, far, far_sems, step, across) for step, (own, far) in enumerate(zip(owns, fars))
        ]
        for copy in fetches:
            copy.start()
        skip_norm(
            half, lat_ref, joint_ref, skip_gain, a_ref, average_ref, inverse_ref,
            send(mine, theirs, stat_sems, 0, other), mine, theirs,
        )
        fetches[0].wait_recv()
    else:
        other = core_pair()
    join_columns(w1, w1o, w1f)

    def rows_of(step, base):
        if tokens_last:
            return a_ref[:, rows_at(step, base)].T
        return a_ref[rows_at(step, base)]

    def give(step):
        at = rows_at(step)
        sent[at] = dot_nn(rows_of(step, half), w1[...])
        send(sent.at[at], got.at[at], sems, step, other).start()

    steps(give, half)
    if not fetch:
        join_rows(w2, w2o, w2f)
    if feed:
        join_rows(w3, w3o, w3f)

    def keep(step):
        at = rows_at(step)
        state = dot_nn(rows_of(step, 0), w1[...])
        if residual:
            state = state + res_ref[at]
        send(sent.at[at], got.at[at], sems, step, other).wait_recv()
        state = state + got[at]
        state_ref[at] = state
        x = row_norm(state)[0] * gain[...]
        if shifted:
            x = x + shift[...]
        x_ref[at] = x.astype(BF16)
        send(x_ref.at[at], x_ref.at[rows_at(step, half)], x_sems, step, other).start()

    steps(keep, half)
    if fetch:
        fetches[1].wait_recv()
        join_rows(w2, w2o, w2f)

    def arrive(step):
        at = rows_at(step)
        send(x_ref.at[at], x_ref.at[rows_at(step, half)], x_sems, step, other).wait_recv()

    if feed:

        def hidden(step, base):
            pre = dot_nn(x_ref[rows_at(step, base)], w2[...])
            return dot_nt(gelu_parts(pre)[0].astype(BF16), w3[...])

        def give_out(step):
            at = rows_at(step)
            arrive(step)
            sent_out[at] = hidden(step, half)
            send(sent_out.at[at], got_out.at[at], out_sems, step, other).start()

        steps(give_out, half)

        def keep_out(step):
            at = rows_at(step)
            value = hidden(step, 0) + state_ref[at]
            send(sent_out.at[at], got_out.at[at], out_sems, step, other).wait_recv()
            out_ref[at] = (value + got_out[at]).astype(BF16)

        steps(keep_out, half)
    else:

        def near_out(step):
            at = rows_at(step)
            out_ref[:, at] = dot_nn(x_ref[at], w2[...]).T

        steps(near_out, half)

        def far_out(step):
            arrive(step)
            at = rows_at(step, half)
            out_ref[:, at] = dot_nn(x_ref[at], w2[...]).T

        steps(far_out, half)

    def drain(step):
        at = rows_at(step)
        send(sent.at[at], got.at[at], sems, step, other).wait_send()
        send(x_ref.at[at], x_ref.at[rows_at(step, half)], x_sems, step, other).wait_send()
        if feed:
            send(sent_out.at[at], got_out.at[at], out_sems, step, other).wait_send()

    steps(drain, half)
    if fetch:
        for copy in fetches[2:]:
            copy.wait_recv()
        for copy in fetches:
            copy.wait_send()


def whole_call(kernel, operands, out_shape, scratch_shapes, collective, name):
    vmem = pl.BlockSpec(memory_space=pltpu.VMEM)
    return pl.pallas_call(
        kernel,
        in_specs=[vmem] * len(operands),
        out_specs=[vmem] * len(out_shape),
        out_shape=[jax.ShapeDtypeStruct(shape, dtype) for shape, dtype in out_shape],
        scratch_shapes=scratch_shapes,
        compiler_params=pltpu.CompilerParams(
            collective_id=collective, has_side_effects=True, vmem_limit_bytes=60 * 2**20
        ),
        cost_estimate=cost(name),
        name=name,
    )(*operands)


def pair_sems(half):
    return pltpu.SemaphoreType.DMA((2, half // CHUNK))


def forward_bridge(a, tokens_last, w1, gain, res, shift, w2, w3, collective, name, later=()):
    fetch = len(later) > 0
    tokens = a[0].shape[0] if fetch else a.shape[1]
    half = tokens // 2
    feed = w3 is not None
    operands = [*(a if fetch else (a,)), *w1, gain]
    operands += [res] if res is not None else []
    operands += [shift] if shift is not None else []
    operands += [*w2, *later] + ([*w3] if feed else [])
    depth, wide = w1[0].shape[0], w2[0].shape[1]
    out_shape = [((half, D), F32), ((tokens, D), BF16)]
    out_shape += [((half, D), BF16)] if feed else [((wide, tokens), F32)]
    part = pltpu.VMEM((half, D), F32)
    joined = [(depth, D), (D, wide)]
    scratch = [part, part, pair_sems(half), pair_sems(half)]
    if fetch:
        out_shape += [((tokens, depth), BF16), ((tokens, 1), F32), ((tokens, 1), F32)]
        out_shape += [(weight.shape, BF16) for weight in later]
        out_shape += [(shape, BF16) for shape in joined]
    else:
        scratch = [pltpu.VMEM(shape, BF16) for shape in joined] + scratch
    if feed:
        scratch += [pltpu.VMEM((D, wide), BF16), part, part, pair_sems(half)]
    if fetch:
        scratch += [
            pltpu.VMEM(w1[0].shape, BF16),
            pltpu.VMEM(w2[0].shape, BF16),
            pltpu.SemaphoreType.DMA((2, 2 + len(later))),
            pltpu.VMEM((tokens, 128), F32),
            pltpu.VMEM((tokens, 128), F32),
            pltpu.SemaphoreType.DMA((2, 1)),
        ]
    return whole_call(
        functools.partial(
            forward_kernel, tokens_last, res is not None, shift is not None, feed, fetch
        ),
        operands,
        out_shape,
        scratch,
        collective,
        name,
    )


def backward_kernel(feed, summed, tokens_last, whole, *refs):
    refs = list(refs)
    take = lambda: refs.pop(0)
    if feed:
        cot_ref, feed_ref, w3o, w3f = take(), take(), take(), take()
    else:
        g_ref, res_ref = take(), take()
    if whole:
        w2, state_ref, gain, w1 = take(), take(), take(), take()
    else:
        w2o, w2f, state_ref, gain, w1o, w1f = (take() for _ in range(6))
    if feed:
        hidden_ref, pre_ref = take(), take()
    total_ref, b_ref, out_ref, gain_ref = take(), take(), take(), take()
    if summed:
        sum_ref = take()
    if not whole:
        w1, w2 = take(), take()
    sent, got, sems, x_sems = take(), take(), take(), take()
    if feed:
        w3 = take()
    half = state_ref.shape[0]
    other = core_pair()
    if not whole:
        join_rows(w2, w2o, w2f)
    if feed:
        join_rows(w3, w3o, w3f)

    def part(step, base):
        at = rows_at(step, base)
        if feed:
            value, slope = gelu_parts(dot_nn(feed_ref[at], w2[...]))
            hidden_ref[at] = value.astype(BF16)
            rows = (dot_nn(cot_ref[at], w3[...]) * slope).astype(BF16)
            pre_ref[at] = rows
        else:
            rows = g_ref[:, at].T
        return dot_nt(rows, w2[...])

    def give(step):
        at = rows_at(step)
        sent[at] = part(step, half)
        send(sent.at[at], got.at[at], sems, step, other).start()

    steps(give, half)
    if not whole:
        join_columns(w1, w1o, w1f)
    gain_ref[...] = jnp.zeros_like(gain_ref)
    if summed:
        sum_ref[...] = jnp.zeros_like(sum_ref)

    def keep(step):
        at = rows_at(step)
        grad = part(step, 0)
        send(sent.at[at], got.at[at], sems, step, other).wait_recv()
        grad = grad + got[at]
        normed, inverse = row_norm(state_ref[at])
        gain_ref[...] += jnp.sum(grad * normed, axis=0, keepdims=True)
        if summed:
            sum_ref[...] += jnp.sum(grad, axis=0, keepdims=True)
        back = row_norm_back(grad, normed, inverse, gain[...])
        total = back + (cot_ref[at].astype(F32) if feed else res_ref[at])
        total_ref[at] = total
        b_ref[at] = total.astype(BF16)
        send(b_ref.at[at], b_ref.at[rows_at(step, half)], x_sems, step, other).start()

    steps(keep, half)

    def product(at):
        value = dot_nt(b_ref[at], w1[...])
        if tokens_last:
            out_ref[:, at] = value.T.astype(out_ref.dtype)
        else:
            out_ref[at] = value.astype(out_ref.dtype)

    def near_out(step):
        product(rows_at(step))

    steps(near_out, half)

    def far_out(step):
        at = rows_at(step)
        send(b_ref.at[at], b_ref.at[rows_at(step, half)], x_sems, step, other).wait_recv()
        product(rows_at(step, half))

    steps(far_out, half)

    def drain(step):
        at = rows_at(step)
        send(sent.at[at], got.at[at], sems, step, other).wait_send()
        send(b_ref.at[at], b_ref.at[rows_at(step, half)], x_sems, step, other).wait_send()

    steps(drain, half)


def backward_bridge(g, res, feed, w2, state, gain, w1, summed, tokens_last, collective, name):
    half = state.shape[0]
    tokens = 2 * half
    depth, wide = w2[0].shape[1], w1[0].shape[0]
    if feed:
        operands = [feed[0], feed[1], *feed[2]]
    else:
        operands = [g, res]
    operands += [*w2, state, gain, *w1]
    out_shape = [((tokens, depth), BF16)] * 2 if feed else []
    out_shape += [((half, D), F32), ((tokens, D), BF16)]
    out_shape += [((wide, tokens), BF16)] if tokens_last else [((tokens, wide), F32)]
    out_shape += [((1, D), F32)] * (2 if summed else 1)
    part = pltpu.VMEM((half, D), F32)
    scratch = [part, part, pair_sems(half), pair_sems(half)]
    whole = len(w1) == 1
    if not whole:
        scratch = [pltpu.VMEM((wide, D), BF16), pltpu.VMEM((D, depth), BF16)] + scratch
    if feed:
        scratch += [pltpu.VMEM((D, depth), BF16)]
    return whole_call(
        functools.partial(backward_kernel, bool(feed), summed, tokens_last, whole),
        operands,
        out_shape,
        scratch,
        collective,
        name,
    )


def product_kernel(by_rows, left_last, left_ref, right_ref, own_ref, far_ref):
    left, right = left_ref[...], right_ref[...]
    if by_rows:
        if left_last:
            value = dot_nn(left, right).T
        else:
            value = dot_tn(right, left)
        value = value.astype(BF16)
        size = value.shape[0] // 2
        parts = (value[:size], value[size:])
    else:
        value = dot_nn(left, right) if left_last else dot_tn(left, right)
        value = value.astype(BF16)
        size = value.shape[1] // 2
        parts = (value[:, :size], value[:, size:])
    for part, ref in zip(parts, (own_ref, far_ref)):
        rows, columns = ref.shape
        if part.shape == ref.shape:
            ref[...] = part
        else:
            ref[:, : columns // 2] = part[:rows]
            ref[:, columns // 2 :] = part[rows:]


def weight_product(left, left_last, right, by_rows, tile, name):
    wide = left.shape[0] if left_last else left.shape[1]
    tokens, across = right.shape
    if left_last:
        left_spec = pl.BlockSpec((tile, tokens), lambda i: (i, 0))
    else:
        left_spec = pl.BlockSpec((tokens, tile), lambda i: (0, i))
    rows = tile * across // 2 // D
    out_spec = pl.BlockSpec((rows, D), lambda i: (i, 0))
    out_shape = jax.ShapeDtypeStruct((rows * (wide // tile), D), BF16)
    return pl.pallas_call(
        functools.partial(product_kernel, by_rows, left_last),
        grid=(wide // tile,),
        in_specs=[left_spec, pl.BlockSpec((tokens, across), lambda i: (0, 0))],
        out_specs=[out_spec, out_spec],
        out_shape=[out_shape, out_shape],
        compiler_params=pltpu.CompilerParams(vmem_limit_bytes=48 * 2**20),
        cost_estimate=cost(name),
        name=name,
    )(left, right)


def pieces_of(rows):
    for pieces in (3, 2, 5):
        if rows % (16 * pieces) == 0:
            return pieces
    return 1


def ring_kernel(size, plan, *refs):
    refs = list(refs)
    sections = len(plan)

    def take(count):
        return [refs.pop(0) for _ in range(count)]

    own_refs = [take(len(parts)) for _, parts in plan]
    far_refs = [take(len(parts)) for _, parts in plan]
    out_refs = take(sections)
    work_refs = take(sections)
    slot_refs = take(sections)
    sends, arrivals, far_sems = take(3)
    index = lax.axis_index("dp")
    chip = lax.axis_index("row")
    core = lax.axis_index("col")
    across = size // 2
    side = lax.rem(index, 2)
    level = index // 2
    place = (1 - side) * level + side * (size - 1 - level)

    def device_at(where):
        where = lax.rem(where + size, size)
        turned = where // across
        high = (1 - turned) * where + turned * (size - 1 - where)
        return (high * 2 + turned, chip, core)

    neighbours = (device_at(place + 1), device_at(place - 1))
    partner = (index, 1 - chip, core)
    barrier = pltpu.get_barrier_semaphore()
    for device in neighbours + (partner,):
        pl.semaphore_signal(barrier, inc=1, device_id=device, device_id_type=MESH)
    pl.semaphore_wait(barrier, 3)

    exchanges = []
    for section in range(sections):
        exchanges.append([])
        if plan[section][0]:
            base = 0
            for number, far in enumerate(far_refs[section]):
                rows = far.shape[0]
                exchange = pltpu.make_async_remote_copy(
                    src_ref=far,
                    dst_ref=work_refs[section].at[base : base + rows],
                    send_sem=far_sems.at[0, section, number],
                    recv_sem=far_sems.at[1, section, number],
                    device_id=partner,
                    device_id_type=MESH,
                )
                exchange.start()
                exchanges[section].append(exchange)
                base += rows

    def ring(which, source, total, slots):
        half = source.shape[0] // 2
        rows = half // size
        pieces = pieces_of(rows)
        piece = rows // pieces

        def span(way, chunk, part):
            chunk = lax.rem(chunk + 2 * size, size)
            return pl.ds(pl.multiple_of(way * half + chunk * rows + part * piece, 16), piece)

        def chunk_of(way, step):
            return place - step if way == 0 else place + step

        def within(part):
            return pl.ds(part * piece, piece)

        def copy(way, part, step, src, dst, phase):
            return pltpu.make_async_remote_copy(
                src_ref=src,
                dst_ref=dst,
                send_sem=sends.at[which, phase, way, part, step],
                recv_sem=arrivals.at[which, phase, way, part, step],
                device_id=neighbours[way],
                device_id_type=MESH,
            )

        def first(way, part):
            src = source.at[span(way, chunk_of(way, 0), part)]
            return copy(way, part, 0, src, slots.at[way, 0, within(part)], 0)

        def reduced(way, part, step):
            src = slots.at[way, step - 1, within(part)]
            return copy(way, part, step, src, slots.at[way, step, within(part)], 0)

        def spread(way, part, step):
            at = span(way, chunk_of(way, step) + (1 if way == 0 else -1), part)
            return copy(way, part, step, total.at[at], total.at[at], 1)

        def arrival(way, part, step):
            return first(way, part) if isinstance(step, int) else reduced(way, part, step)

        def added(way, part, step):
            at = span(way, chunk_of(way, step + 1), part)
            got = slots[way, step, within(part)]
            return at, (source[at].astype(F32) + got.astype(F32)).astype(BF16)

        each = [(way, part) for part in range(pieces) for way in range(2)]
        for way, part in each:
            first(way, part).start()

        def reduce_step(step, carry):
            for way, part in each:
                arrival(way, part, step).wait_recv()
                _, value = added(way, part, step)
                slots[way, step, within(part)] = value
                reduced(way, part, step + 1).start()
            return carry

        reduce_step(0, 0)
        lax.fori_loop(1, size - 2, reduce_step, 0)
        for way, part in each:
            reduced(way, part, size - 2).wait_recv()
            at, value = added(way, part, size - 2)
            total[at] = value
            spread(way, part, 0).start()

        def gather_step(step, carry):
            for way, part in each:
                spread(way, part, step).wait_recv()
                spread(way, part, step + 1).start()
            return carry

        lax.fori_loop(0, size - 2, gather_step, 0)
        for way, part in each:
            spread(way, part, size - 2).wait_recv()
            first(way, part).wait_send()
            spread(way, part, 0).wait_send()

        def drain(step, carry):
            for way, part in each:
                reduced(way, part, step).wait_send()
                spread(way, part, step).wait_send()
            return carry

        lax.fori_loop(1, size - 1, drain, 0)

    for section in range(sections):
        exchanged, parts = plan[section]
        work = work_refs[section]
        base = 0
        for number, rows in enumerate(parts):
            own = own_refs[section][number][...]
            if exchanged:
                exchanges[section][number].wait()
                near = work[base : base + rows]
            else:
                near = far_refs[section][number][...]
            work[base : base + rows] = (own.astype(F32) + near.astype(F32)).astype(BF16)
            base += rows
        if base < work.shape[0]:
            work[base:] = jnp.zeros((work.shape[0] - base, work.shape[1]), BF16)
        ring(section, work, out_refs[section], slot_refs[section])


def ring_sum(size, sections):
    vmem = pl.BlockSpec(memory_space=pltpu.VMEM)
    plan = tuple((exchanged, tuple(own.shape[0] for own in owns)) for exchanged, owns, _ in sections)
    owns = [own for _, parts, _ in sections for own in parts]
    fars = [far for _, _, parts in sections for far in parts]
    totals = [sum(parts) for _, parts in plan]
    totals = [rows + -rows % (32 * size) for rows in totals]
    whole = [pltpu.VMEM((rows, D), BF16) for rows in totals]
    slots = [pltpu.VMEM((2, size - 1, rows // 2 // size, D), BF16) for rows in totals]
    pieces = max(pieces_of(rows // 2 // size) for rows in totals)
    sems = pltpu.SemaphoreType.DMA((len(sections), 2, 2, pieces, size - 1))
    most = max(len(parts) for _, parts in plan)
    return pl.pallas_call(
        functools.partial(ring_kernel, size, plan),
        in_specs=[vmem] * (len(owns) + len(fars)),
        out_specs=[vmem] * len(sections),
        out_shape=[jax.ShapeDtypeStruct((rows, D), BF16) for rows in totals],
        scratch_shapes=whole
        + slots
        + [sems, sems, pltpu.SemaphoreType.DMA((2, len(sections), most))],
        compiler_params=pltpu.CompilerParams(
            collective_id=0, has_side_effects=True, vmem_limit_bytes=62 * 2**20
        ),
        cost_estimate=cost("ring_sum"),
        name="ring_sum",
    )(*owns, *fars)


def shards(
    latents,
    skip_input,
    condition,
    text_states,
    positions,
    cotangent,
    skip_gain,
    skip_weight,
    shift_weight,
    self_gain,
    self_weight,
    query_gain,
    key_gain,
    self_out,
    cross_gain,
    cross_query,
    cross_context,
    cross_query_gain,
    cross_key_gain,
    cross_out,
    feed_gain,
    up_weight,
    down_weight,
):
    tokens, width = latents.shape
    half = tokens // 2
    heads_here = width // HD
    core = lax.axis_index("col")
    chip = lax.axis_index("row")
    straight = core == chip

    def own_first(values):
        return (
            lax.dynamic_slice_in_dim(values, core * half, half, 0),
            lax.dynamic_slice_in_dim(values, (1 - core) * half, half, 0),
        )

    def in_order(own, other):
        return jnp.where(
            core == 0, jnp.concatenate([own, other]), jnp.concatenate([other, own])
        )

    skip_flat = skip_weight.reshape(2 * width, -1)
    self_flat = self_weight.reshape(-1, 3 * width)
    context_flat = cross_context.reshape(-1, 2 * width)

    rows = up_weight.shape[0]
    norm_far = other_chip(jnp.stack([self_gain, cross_gain, feed_gain]))

    def near_and_far(weight):
        return (weight, other_chip(weight))

    def share_of(weight):
        share = weight.shape[0] // lax.axis_size("dp")
        piece = lax.dynamic_slice_in_dim(weight, lax.axis_index("dp") * share, share, 0)
        return other_chip(piece)

    down_turned = down_weight.T
    up_share, down_share = share_of(up_weight), share_of(down_turned)
    up_pair = (up_weight, lax.all_gather(up_share, "dp", axis=0, tiled=True))
    down_pair = (down_turned, lax.all_gather(down_share, "dp", axis=0, tiled=True))
    norm_gains = jnp.concatenate([jnp.stack([self_gain, cross_gain, feed_gain]), norm_far], axis=1)
    self_gain_all, cross_gain_all, feed_gain_all = norm_gains[0:1], norm_gains[1:2], norm_gains[2:3]

    text_near = other_core(text_states)
    text_mine = jnp.where(straight, text_states, text_near)
    text_here = text_states.shape[0]
    kept, handed = own_first(cotangent)
    handed = other_core(handed)
    cot_mine = jnp.where(straight, kept, handed)

    place_own, place_other = own_first(positions)
    places = jnp.concatenate([place_own, place_other]).astype(F32)
    quarter = HD // 4
    frequency = 10000.0 ** (-jnp.arange(quarter, dtype=F32) / quarter)
    angles = frequency[:, None] * places.T[:, None, :]
    cosine = jnp.cos(angles)
    sine = jnp.sin(angles)
    cosine = jnp.stack([cosine, cosine], axis=1).reshape(HD, tokens)
    sine = jnp.stack([-sine, sine], axis=1).reshape(HD, tokens)

    lat_own, lat_other = own_first(latents)
    skip_own, skip_other = own_first(skip_input)
    lat = jnp.concatenate([lat_own, lat_other]).astype(F32)
    joint = jnp.concatenate([skip_own, skip_other]).astype(F32)

    def swap_halves(values):
        return jnp.concatenate([values[:, half:], values[:, :half]], axis=1)

    cond_low = jax.nn.silu(condition.astype(F32)).astype(BF16)
    shift_part = contract(cond_low, shift_weight)
    shift_part = shift_part + other_core(shift_part)
    shift_mine = lax.dynamic_slice_in_dim(shift_part, chip, 1, 0)
    shift_far = other_chip(lax.dynamic_slice_in_dim(shift_part, 1 - chip, 1, 0))
    shift_row = jnp.concatenate([shift_mine, shift_far], axis=1)

    (
        first_state,
        first_all,
        mixed_raw,
        skip_low,
        average,
        skip_inverse,
        out_far_half,
        query_far_half,
        skip_whole,
        self_whole,
    ) = forward_bridge(
        (latents, skip_input, skip_gain), False, (skip_flat,), self_gain_all, None, shift_row, (self_flat,), None, 1, "into_self",
        (self_out, cross_query),
    )
    mixed_raw = mixed_raw.reshape(3 * heads_here, HD, tokens)


    def fetched(values, gate):
        return other_chip(after(values, gate))

    out_pair = (self_out, out_far_half)
    query_pair = (cross_query, query_far_half)
    text_far = fetched(jnp.where(straight, text_near, text_states), first_all)
    context_far = fetched(context_flat, text_far)
    cross_pair = (cross_out, fetched(cross_out, text_far))
    mixed_raw = after(mixed_raw, text_far)
    self_args = (
        (mixed_raw, mixed_raw, mixed_raw),
        (0, heads_here, 2 * heads_here),
        heads_here,
        query_gain[:, None],
        key_gain[:, None],
        (cosine, sine),
        tokens,
    )
    heads_low, log_first = attend(*self_args[0], *self_args[1:])
    heads_flat = heads_low.reshape(width, tokens)
    cot_far = fetched(jnp.where(straight, handed, kept), heads_low)
    second_state, cross_all, probe_raw = forward_bridge(
        heads_flat, True, out_pair, cross_gain_all, first_state, None, query_pair, None, 2, "into_cross"
    )
    probe_raw = probe_raw.reshape(heads_here, HD, tokens)
    text_far, context_far = after((text_far, context_far), cross_all)
    text_all = jnp.concatenate([text_mine, text_far], axis=1)
    text_all = jnp.pad(text_all, ((0, -text_here % 128), (0, 0)))
    context_all = jnp.concatenate([context_flat, context_far])
    memory_raw = lax.dot_general(
        context_all, text_all, (((0,), (1,)), ((), ())), preferred_element_type=F32
    ).reshape(2 * heads_here, HD, -1)
    cross_args = (
        (probe_raw, memory_raw, memory_raw),
        (0, 0, heads_here),
        heads_here,
        cross_query_gain[:, None],
        cross_key_gain[:, None],
        (),
        text_here,
    )
    cross_low, log_second = attend(*cross_args[0], *cross_args[1:])
    cross_flat = cross_low.reshape(width, tokens)
    third_state, feed_all, out_own = forward_bridge(
        cross_flat, True, cross_pair, feed_gain_all, second_state, None, up_pair, down_pair, 3, "into_feed"
    )
    row_width = up_weight.shape[0]
    out_mine = out_own[:, :row_width]
    out_far = other_chip(out_own[:, row_width:])

    cot_own = jnp.concatenate([cot_mine, after(cot_far, feed_all)], axis=1)
    cot_all = pair(cot_own)
    (
        hidden_low,
        grad_pre,
        grad_third,
        branch_two_all,
        grad_cross_heads,
        feed_gain_part,
    ) = backward_bridge(
        None,
        None,
        (cot_all, feed_all, down_pair),
        up_pair,
        third_state,
        feed_gain_all,
        cross_pair,
        False,
        True,
        4,
        "from_feed",
    )
    down_own, down_far = weight_product(hidden_low, False, cot_all, True, 1152, "grad_down")
    up_own, up_far = weight_product(grad_pre, False, feed_all, True, 1152, "grad_up")
    cross_own, cross_far = weight_product(
        cross_flat, True, branch_two_all, False, 576, "grad_cross_out"
    )
    down_far_here = other_chip(down_far)
    up_far_here = other_chip(up_far)
    grad_cross_heads = after(grad_cross_heads, (down_far, up_far))
    grad_probe, grad_memory, grad_cross_gains = attend_back(
        *cross_args[0],
        *cross_args[1:],
        cross_low,
        log_second,
        grad_cross_heads.reshape(heads_here, HD, tokens),
    )
    probe_low = grad_probe.reshape(width, tokens)
    query_own, query_far = weight_product(probe_low, True, cross_all, True, 576, "grad_cross_query")
    memory_low = grad_memory.reshape(2 * width, -1)
    context_own, context_far = weight_product(
        memory_low, True, text_all, True, 576, "grad_context"
    )
    early_own = jnp.concatenate([cross_own, query_own, context_own])
    early_far = jnp.concatenate([cross_far, query_far, context_far])
    early_here = other_chip(early_far)
    probe_low = after(probe_low, early_far)
    text_part = lax.dot_general(
        memory_low, context_all, (((0,), (1,)), ((), ())), preferred_element_type=F32
    )[:text_here]
    text_width = text_states.shape[1]
    text_one, text_two = text_part[:, :text_width], text_part[:, text_width:]
    text_sum = jnp.where(straight, text_one, text_two) + other_core(
        jnp.where(straight, text_two, text_one)
    )
    text_sum = text_sum.astype(BF16)
    text_back = lax.ppermute(text_sum, ("row", "col"), [(1, 2), (2, 1)])

    grad_second, branch_one_all, grad_heads, cross_gain_part = backward_bridge(
        probe_low,
        grad_third,
        None,
        query_pair,
        second_state,
        cross_gain_all,
        out_pair,
        False,
        True,
        5,
        "from_cross",
    )
    out_grad_own, out_grad_far = weight_product(
        heads_flat, True, branch_one_all, False, 576, "grad_self_out"
    )

    def summed(own, far):
        return (own.astype(F32) + far.astype(F32)).astype(BF16)

    down_sum = summed(down_own, after(down_far_here, grad_heads))
    down_share = lax.psum_scatter(down_sum, "dp", scatter_dimension=0, tiled=True)
    grad_heads_in = after(grad_heads, down_sum)
    grad_mixed, grad_self_gains = attend_back(
        *self_args[0],
        *self_args[1:],
        heads_low,
        log_first,
        grad_heads_in.reshape(heads_here, HD, tokens),
    )
    mixed_low = grad_mixed.reshape(3 * width, tokens)
    up_sum = summed(up_own, up_far_here)
    mixed_in = after(mixed_low, (down_share, up_sum))
    self_own, self_far = weight_product(mixed_low, True, first_all, True, 576, "grad_self")
    _, grad_first_all, grad_skip_out, self_gain_part, shift_grad = backward_bridge(
        mixed_in,
        grad_second,
        None,
        (self_whole,),
        first_state,
        self_gain_all,
        (skip_whole,),
        True,
        False,
        6,
        "from_self",
    )
    skip_own, skip_far = weight_product(skip_low, False, grad_first_all, False, 384, "grad_skip")
    shift_grad = shift_grad + other_core(shift_grad)
    shift_here = shift_grad[:, :row_width]
    shift_there = other_chip(shift_grad[:, row_width:])
    shift_pair = jnp.where(
        chip == 0,
        jnp.concatenate([shift_here, shift_there]),
        jnp.concatenate([shift_there, shift_here]),
    )
    out_far = after(out_far, grad_skip_out)
    out_kept = jnp.where(straight, out_mine, out_far)
    out_got = other_core(jnp.where(straight, out_far, out_mine))
    block_out = in_order(out_kept, out_got)
    lat_normed = (lat - average) * skip_inverse
    joint_normed = (joint - average) * skip_inverse
    grad_lat, grad_joint = grad_skip_out[:, :width], grad_skip_out[:, width:]
    lat_scaled, joint_scaled = grad_lat * skip_gain[0], grad_joint * skip_gain[1]
    sums_back = jnp.stack(
        [
            jnp.sum(lat_scaled, axis=1) + jnp.sum(joint_scaled, axis=1),
            jnp.sum(lat_scaled * lat_normed, axis=1) + jnp.sum(joint_scaled * joint_normed, axis=1),
        ]
    )
    sums_back = sums_back + swap_halves(other_core(sums_back))
    first_mean = (sums_back[0] / (2 * D))[:, None]
    second_mean = (sums_back[1] / (2 * D))[:, None]
    skip_gain_part = jnp.stack(
        [jnp.sum(grad_lat * lat_normed, axis=0), jnp.sum(grad_joint * joint_normed, axis=0)]
    )
    grad_lat = (skip_inverse * (lat_scaled - first_mean - lat_normed * second_mean)).astype(BF16)
    grad_joint = (skip_inverse * (joint_scaled - first_mean - joint_normed * second_mean)).astype(BF16)
    grad_latents = in_order(grad_lat[:half], grad_lat[half:])
    grad_skip_input = in_order(grad_joint[:half], grad_joint[half:])

    wide = jnp.concatenate([self_gain_part, cross_gain_part, feed_gain_part])
    wide = wide + other_core(wide)
    narrow = jnp.concatenate([jnp.sum(grad_self_gains, axis=0), jnp.sum(grad_cross_gains, axis=0)])
    narrow = narrow[:, :, 0]
    narrow = narrow + other_core(narrow)

    def flat(*pieces):
        return jnp.concatenate([piece.reshape(-1) for piece in pieces])

    kept_gains = flat(wide[:, :row_width], narrow, skip_gain_part)
    sent_gains = flat(wide[:, row_width:], narrow, skip_gain_part)
    small = flat(
        kept_gains + other_chip(sent_gains), cond_low.astype(F32), shift_pair
    )
    groups = lax.axis_size("dp")
    smalls = [small] + [
        lax.ppermute(small, "dp", [(i, (i + k) % groups) for i in range(groups)])
        for k in range(1, groups)
    ]
    skip_own = after(skip_own, (grad_latents, grad_skip_input, block_out, small))
    middle, inner, last = ring_sum(
        groups,
        [
            (False, [early_own], [early_here]),
            (True, [out_grad_own, self_own], [out_grad_far, self_far]),
            (True, [skip_own], [skip_far]),
        ],
    )
    high = lax.psum(up_sum, "dp")
    low = lax.all_gather(down_share, "dp", axis=0, tiled=True)

    def unpack(block, count):
        rows = block.shape[0] // count
        pieces = [block[i * rows : (i + 1) * rows] for i in range(count)]
        return [
            jnp.concatenate([piece[:, :width], piece[:, width:]]).astype(F32) for piece in pieces
        ]


    def side_by_side(blocks):
        return jnp.concatenate([blocks[:row_width], blocks[row_width:]], axis=1).astype(F32)

    grad_down = side_by_side(low).T
    grad_up = side_by_side(high)
    place = width // 2
    grad_cross_out, grad_cross_query = unpack(middle[: 2 * place], 2)
    grad_context = jnp.concatenate(unpack(middle[2 * place : 2 * place + text_width], 2), axis=1)
    (grad_self_out,) = unpack(inner[:place], 1)
    grad_self_weight = jnp.stack(unpack(inner[place : 4 * place], 3), axis=1)
    grad_skip_weight = jnp.concatenate(unpack(last[: 2 * place], 3))

    grad_text_states = jnp.where(straight, text_sum, after(text_back, last))

    smalls = [after(value, last) for value in smalls[1:]] + smalls[:1]
    gain_count = kept_gains.shape[0]
    gain_sums = sum(value[:gain_count] for value in smalls)
    images = condition.shape[0]
    conds = [
        value[gain_count : gain_count + images * width].reshape(images, width) for value in smalls
    ]
    shifts = [value[gain_count + images * width :].reshape(images, row_width) for value in smalls]
    grad_shift_weight = lax.dot_general(
        jnp.concatenate(conds),
        jnp.concatenate(shifts),
        (((0,), (0,)), ((), ())),
        precision=PRECISE,
        preferred_element_type=F32,
    )
    wide_sum = gain_sums[: 3 * row_width].reshape(3, row_width)
    narrow_sum = gain_sums[3 * row_width : 3 * row_width + 4 * HD].reshape(4, HD)
    grad_skip_gain = gain_sums[3 * row_width + 4 * HD :].reshape(2, width)

    return (
        block_out,
        grad_latents,
        grad_skip_input,
        grad_text_states,
        grad_skip_gain,
        grad_skip_weight.reshape(skip_weight.shape),
        grad_shift_weight,
        wide_sum[0],
        grad_self_weight.reshape(self_weight.shape),
        narrow_sum[0],
        narrow_sum[1],
        grad_self_out,
        wide_sum[1],
        grad_cross_query,
        grad_context.reshape(cross_context.shape),
        narrow_sum[2],
        narrow_sum[3],
        grad_cross_out,
        wide_sum[2],
        grad_up,
        grad_down,
    )


def solution(mesh):
    placed = (
        P(("dp", "row"), "col"),
        P(("dp", "row"), "col"),
        P("dp", "col"),
        P(("dp", "col"), "row"),
        P(("dp", "row"), None),
        P(("dp", "col"), "row"),
        P(None, "col"),
        P(None, "col", "row"),
        P("col", "row"),
        P("row"),
        P("row", None, "col"),
        P(),
        P(),
        P("col", "row"),
        P("row"),
        P("row", "col"),
        P("row", None, "col"),
        P(),
        P(),
        P("col", "row"),
        P("row"),
        P("row", "col"),
        P("col", "row"),
    )
    return jax.shard_map(
        shards,
        mesh=mesh,
        in_specs=placed,
        out_specs=(
            P(("dp", "col"), "row"),
            P(("dp", "row"), "col"),
            P(("dp", "row"), "col"),
            P(("dp", "col"), "row"),
            P(None, "col"),
            P(None, "col", "row"),
            P("col", "row"),
            P("row"),
            P("row", None, "col"),
            P(),
            P(),
            P("col", "row"),
            P("row"),
            P("row", "col"),
            P("row", None, "col"),
            P(),
            P(),
            P("col", "row"),
            P("row"),
            P("row", "col"),
            P("col", "row"),
        ),
        check_vma=False,
    )
```
